32 devices in a mesh: mp: 4 (over x, core), dp: 8 (over z, y).
Axes of the slice: x: 2, y: 2, z: 4, core: 2. Of those that a mesh axis runs over, the one named last changes fastest.
Arguments:
- tokens: bfloat16 [2048, 2048], P('dp'), may hold values from -7 to 7
- cotangent: bfloat16 [2048, 2048], P('dp'), may hold values from -6 to 6
- token_sequence_index: int32 [2048], P('dp'), may hold values from 0 to 1, as said below
- positions: int32 [2048], P('dp'), may hold values from 0 to 1023, as said below
- token_exit_loop: int32 [2048], P('dp'), may hold values from 0 to 2
- current_loop: int32 [1], replicated, may hold values from 0 to 2
- attention_norm_gain: float32 [2048], replicated, may hold values from 0.1 to 1.9
- feedforward_norm_gain: float32 [2048], replicated, may hold values from 0.1 to 1.9
- probe: float32 [2048], replicated, may hold values from -0.125 to 0.125
- query_matrix: bfloat16 [2048, 2048], P('dp', 'mp'), may hold values from -0.125 to 0.125
- key_value_matrix: bfloat16 [2048, 512], P('dp'), may hold values from -0.125 to 0.125
- output_matrix: bfloat16 [2048, 2048], P('dp', 'mp'), may hold values from -0.5 to 0.5
- gate_matrix: bfloat16 [2048, 16384], P('dp', 'mp'), may hold values from -0.125 to 0.125
- up_matrix: bfloat16 [2048, 16384], P('dp', 'mp'), may hold values from -0.125 to 0.125
- down_matrix: bfloat16 [2048, 16384], P('dp', 'mp'), may hold values from -0.046875 to 0.046875
- query_update_left: bfloat16 [3, 2048, 256], P(None, 'dp'), may hold values from -0.125 to 0.125
- query_update_right: bfloat16 [3, 256, 2048], P(None, None, 'mp'), may hold values from -0.375 to 0.375
- key_value_update_left: bfloat16 [3, 2048, 512], P(None, 'dp'), may hold values from -0.125 to 0.125
- key_value_update_right: bfloat16 [3, 256, 512], replicated, may hold values from -0.375 to 0.375
- output_update_left: bfloat16 [3, 2048, 256], P(None, 'dp'), may hold values from -0.5 to 0.5
- output_update_right: bfloat16 [3, 256, 2048], P(None, None, 'mp'), may hold values from -0.375 to 0.375
- gate_update_left: bfloat16 [3, 2048, 256], P(None, 'dp'), may hold values from -0.125 to 0.125
- gate_update_right: bfloat16 [3, 256, 16384], P(None, None, 'mp'), may hold values from -0.375 to 0.375
- up_update_left: bfloat16 [3, 2048, 256], P(None, 'dp'), may hold values from -0.125 to 0.125
- up_update_right: bfloat16 [3, 256, 16384], P(None, None, 'mp'), may hold values from -0.375 to 0.375
- down_update_left: bfloat16 [3, 2048, 256], P(None, 'dp'), may hold values from -0.046875 to 0.046875
- down_update_right: bfloat16 [3, 256, 16384], P(None, None, 'mp'), may hold values from -0.375 to 0.375
Outputs:
- counts: int32 [3], replicated
- confidence: float32 [1], replicated
- mixed: bfloat16 [2048, 2048], P('dp')
- tokens_grad: float32 [2048, 2048], P('dp')
- attn_gain_grad: float32 [2048], P('dp')
- mlp_gain_grad: float32 [2048], P('dp')
- q_weight_grad: float32 [2048, 2048], P('dp', 'mp')
- kv_weight_grad: float32 [2048, 512], P('dp')
- o_weight_grad: float32 [2048, 2048], P('dp', 'mp')
- gate_weight_grad: float32 [2048, 16384], P('dp', 'mp')
- up_weight_grad: float32 [2048, 16384], P('dp', 'mp')
- down_weight_grad: float32 [2048, 16384], P('dp', 'mp')
- q_lora_a_grad: float32 [3, 2048, 256], P(None, 'dp')
- q_lora_b_grad: float32 [3, 256, 2048], P(None, 'dp', 'mp')
- kv_lora_a_grad: float32 [3, 2048, 512], P(None, 'dp')
- kv_lora_b_grad: float32 [3, 256, 512], P(None, 'dp')
- o_lora_a_grad: float32 [3, 2048, 256], P(None, 'dp')
- o_lora_b_grad: float32 [3, 256, 2048], P(None, 'dp', 'mp')
- gate_lora_a_grad: float32 [3, 2048, 256], P(None, 'dp')
- gate_lora_b_grad: float32 [3, 256, 16384], P(None, 'dp', 'mp')
- up_lora_a_grad: float32 [3, 2048, 256], P(None, 'dp')
- up_lora_b_grad: float32 [3, 256, 16384], P(None, 'dp', 'mp')
- down_lora_a_grad: float32 [3, 2048, 256], P(None, 'dp')
- down_lora_b_grad: float32 [3, 256, 16384], P(None, 'dp', 'mp')
The draws below stay inside these ranges and needn't reach their ends.
Inputs may be any that keep to these rules, and one draw needn't show every extreme that they name: `token_sequence_index`: sequence 0 has 1024 tokens, in two blocks of 64 consecutive positions in every block of 256 tokens; the other sequences have 1024 tokens each, packed in order into the remaining half of the blocks. Each pair of sequence and position occurs once; positions of a sequence run from 0 to its length less one.
All inputs are finite; a program needn't handle non-finite values.
Results may differ from the reference program's by a relative error of at most 0.015.
The reference program's roundings to bfloat16 on the way count: a program that leaves them out, or rounds other values in their place, can miss the bound.
Values may be sent and summed in bfloat16 or wider, within the bound.
No kernel may reach another device: no remote copies, remote signals or barrier semaphores. Data moves between devices by JAX's collectives and lax.ppermute only.
A program may use at most 768 MiB of HBM per device.

```python
import math
import jax
import jax.numpy as jnp
from jax import lax

MODEL_WIDTH = 2048
HQ = 8
HEAD_SIZE = 256
HIDDEN_UNITS = 16384
UPDATE_RANK = 256
LOOP_COUNT = 3
TOK_DEV = 256
TOKENS = 2048
SEQ_LEN = 1024
QUERY_WIDTH = 2048


def layout(key):
    devices = TOKENS // TOK_DEV
    quarter = TOK_DEV // 4
    half_rows = TOK_DEV // 2
    order = jax.random.permutation(jax.random.fold_in(key, 7), devices).astype(jnp.int32)
    flips = jax.random.randint(jax.random.fold_in(key, 5), (devices, 1), 0, 2)
    slots = jnp.arange(quarter, dtype=jnp.int32)
    first_spots = order[:, None] * quarter + slots[None, :]
    second_spots = (2 * devices - 1 - order)[:, None] * quarter + slots[None, :]
    packed = jnp.arange(devices, dtype=jnp.int32)[:, None] * half_rows + jnp.arange(half_rows, dtype=jnp.int32)[None, :]
    long_ids = jnp.zeros((devices, half_rows), jnp.int32)
    long_spots = jnp.concatenate([first_spots, second_spots], axis=1)
    short_ids = 1 + packed // SEQ_LEN
    short_spots = packed % SEQ_LEN
    ids_front = jnp.concatenate([long_ids, short_ids], axis=1)
    ids_rear = jnp.concatenate([short_ids, long_ids], axis=1)
    spots_front = jnp.concatenate([long_spots, short_spots], axis=1)
    spots_rear = jnp.concatenate([short_spots, long_spots], axis=1)
    ids_all = jnp.where(flips == 1, ids_rear, ids_front).reshape(TOKENS)
    spots_all = jnp.where(flips == 1, spots_rear, spots_front).reshape(TOKENS)
    return (ids_all, spots_all)


def draw_token_sequence_index(key, part):
    ids_all, spots_all = layout(key)
    return ids_all


def draw_positions(key, part):
    ids_all, spots_all = layout(key)
    return spots_all


def draw_tokens(key, part):
    key = jax.random.fold_in(key, 3)
    noise_key, offset_key = jax.random.split(key)
    noise = jax.random.truncated_normal(noise_key, -4.0, 4.0, (TOKENS, MODEL_WIDTH), jnp.float32)
    offset = jax.random.truncated_normal(offset_key, -3.0, 3.0, (MODEL_WIDTH,), jnp.float32)
    return (noise + offset[None, :]).astype(jnp.bfloat16)


def plant(result, stream_key, smallest, largest):
    place = [jax.random.randint(jax.random.fold_in(stream_key, axis), (), 0, length) for axis, length in enumerate(result.shape)]
    widest = result.shape.index(max(result.shape))
    neighbour = place[:widest] + [(place[widest] + 1) % result.shape[widest]] + place[widest + 1:]
    return result.at[tuple(place)].set(smallest).at[tuple(neighbour)].set(largest)


def steps_of(key, shape, cuts, least, high):
    loudness = 1.0
    for dim, blocks in cuts:
        draws = jax.random.uniform(jax.random.fold_in(jax.random.fold_in(key, 6), dim), (blocks,), jnp.float32, least / len(cuts), high / len(cuts))
        loudness = loudness * jnp.repeat(jnp.exp(draws), shape[dim] // blocks).reshape((-1,) + (1,) * (len(shape) - 1 - dim))
    return loudness


def normal_values(own_key, dims, width, bound, cuts=(), kind=jnp.bfloat16):
    level = steps_of(own_key, dims, cuts, -0.22, 0.18) if cuts else 1.0
    array = jax.random.normal(own_key, dims, jnp.float32) * width * level
    return jnp.minimum(jnp.maximum(array, -bound), bound).astype(kind)


def setup_inputs(seed: int = 0) -> dict:
    arg_keys = jax.random.split(jax.random.key(seed), 28)
    tokens = draw_tokens(jax.random.fold_in(arg_keys[27], 71), 0)
    cotangent = normal_values(arg_keys[1], (TOKENS, MODEL_WIDTH), 1.0, 6.0, ((0, 8),))
    token_sequence_index = draw_token_sequence_index(jax.random.fold_in(arg_keys[27], 71), 0)
    positions = draw_positions(jax.random.fold_in(arg_keys[27], 71), 0)
    token_exit_loop = plant(jax.random.randint(arg_keys[4], (TOKENS,), 0, LOOP_COUNT), jax.random.fold_in(arg_keys[4], 1), 0, LOOP_COUNT - 1).astype(jnp.int32)
    current_loop = jax.random.randint(arg_keys[5], (1,), 0, LOOP_COUNT).astype(jnp.int32)
    attention_norm_gain = jnp.clip(1.0 + 0.18 * jax.random.normal(arg_keys[6], (MODEL_WIDTH,), jnp.float32), 0.1, 1.9)
    feedforward_norm_gain = jnp.clip(1.0 + 0.18 * jax.random.normal(arg_keys[7], (MODEL_WIDTH,), jnp.float32), 0.1, 1.9)
    probe = normal_values(arg_keys[8], (MODEL_WIDTH,), MODEL_WIDTH ** -0.5, 0.125, (), jnp.float32)
    query_matrix = normal_values(arg_keys[9], (MODEL_WIDTH, QUERY_WIDTH), MODEL_WIDTH ** -0.5, 0.125, ((0, 8), (1, 4)))
    key_value_matrix = normal_values(arg_keys[10], (MODEL_WIDTH, 2 * HEAD_SIZE), MODEL_WIDTH ** -0.5, 0.125, ((0, 8),))
    output_matrix = normal_values(arg_keys[11], (MODEL_WIDTH, QUERY_WIDTH), (QUERY_WIDTH // 16) ** -0.5, 0.5, ((0, 8), (1, 4)))
    gate_matrix = normal_values(arg_keys[12], (MODEL_WIDTH, HIDDEN_UNITS), MODEL_WIDTH ** -0.5, 0.125, ((0, 8), (1, 4)))
    up_matrix = normal_values(arg_keys[13], (MODEL_WIDTH, HIDDEN_UNITS), MODEL_WIDTH ** -0.5, 0.125, ((0, 8), (1, 4)))
    down_matrix = normal_values(arg_keys[14], (MODEL_WIDTH, HIDDEN_UNITS), HIDDEN_UNITS ** -0.5, 0.046875, ((0, 8), (1, 4)))
    query_update_left = normal_values(arg_keys[15], (LOOP_COUNT, MODEL_WIDTH, UPDATE_RANK), MODEL_WIDTH ** -0.5, 0.125, ((1, 8),))
    query_update_right = normal_values(arg_keys[16], (LOOP_COUNT, UPDATE_RANK, QUERY_WIDTH), UPDATE_RANK ** -0.5, 0.375, ((2, 4),))
    key_value_update_left = normal_values(arg_keys[17], (LOOP_COUNT, MODEL_WIDTH, 2 * UPDATE_RANK), MODEL_WIDTH ** -0.5, 0.125, ((1, 8),))
    key_value_update_right = normal_values(arg_keys[18], (LOOP_COUNT, UPDATE_RANK, 2 * HEAD_SIZE), UPDATE_RANK ** -0.5, 0.375)
    output_update_left = normal_values(arg_keys[19], (LOOP_COUNT, MODEL_WIDTH, UPDATE_RANK), (QUERY_WIDTH // 16) ** -0.5, 0.5, ((1, 8),))
    output_update_right = normal_values(arg_keys[20], (LOOP_COUNT, UPDATE_RANK, QUERY_WIDTH), UPDATE_RANK ** -0.5, 0.375, ((2, 4),))
    gate_update_left = normal_values(arg_keys[21], (LOOP_COUNT, MODEL_WIDTH, UPDATE_RANK), MODEL_WIDTH ** -0.5, 0.125, ((1, 8),))
    gate_update_right = normal_values(arg_keys[22], (LOOP_COUNT, UPDATE_RANK, HIDDEN_UNITS), UPDATE_RANK ** -0.5, 0.375, ((2, 4),))
    up_update_left = normal_values(arg_keys[23], (LOOP_COUNT, MODEL_WIDTH, UPDATE_RANK), MODEL_WIDTH ** -0.5, 0.125, ((1, 8),))
    up_update_right = normal_values(arg_keys[24], (LOOP_COUNT, UPDATE_RANK, HIDDEN_UNITS), UPDATE_RANK ** -0.5, 0.375, ((2, 4),))
    down_update_left = normal_values(arg_keys[25], (LOOP_COUNT, MODEL_WIDTH, UPDATE_RANK), HIDDEN_UNITS ** -0.5, 0.046875, ((1, 8),))
    down_update_right = normal_values(arg_keys[26], (LOOP_COUNT, UPDATE_RANK, HIDDEN_UNITS), UPDATE_RANK ** -0.5, 0.375, ((2, 4),))
    return dict(tokens=tokens, cotangent=cotangent, token_sequence_index=token_sequence_index, positions=positions, token_exit_loop=token_exit_loop, current_loop=current_loop, attention_norm_gain=attention_norm_gain, feedforward_norm_gain=feedforward_norm_gain, probe=probe, query_matrix=query_matrix, key_value_matrix=key_value_matrix, output_matrix=output_matrix, gate_matrix=gate_matrix, up_matrix=up_matrix, down_matrix=down_matrix, query_update_left=query_update_left, query_update_right=query_update_right, key_value_update_left=key_value_update_left, key_value_update_right=key_value_update_right, output_update_left=output_update_left, output_update_right=output_update_right, gate_update_left=gate_update_left, gate_update_right=gate_update_right, up_update_left=up_update_left, up_update_right=up_update_right, down_update_left=down_update_left, down_update_right=down_update_right)


@jax.custom_vjp
def low(v):
    return lax.optimization_barrier(v.astype(jnp.bfloat16)).astype(jnp.float32)

@jax.custom_vjp
def low_back(v):
    return v

def low_keep(v):
    return (low(v), None)

def low_pass(kept, grad):
    return (grad,)

def back_keep(v):
    return (v, None)

def back_low(kept, grad):
    return (low(grad),)
low.defvjp(low_keep, low_pass)
low_back.defvjp(back_keep, back_low)
precise = lax.Precision.HIGHEST
EPSILON = 1e-06
MASKED_SCORE = -1e+30

def matmul(left_factor, right_factor):
    return jnp.dot(left_factor, right_factor, precision=precise)

def rms_norm(inputs, gain):
    return inputs * lax.rsqrt(lax.optimization_barrier(jnp.mean(inputs * inputs, axis=-1, keepdims=True)) + EPSILON) * gain

def rotate(inputs, spots, direction):
    half_width = inputs.shape[-1] // 2
    frequency = jnp.exp(jnp.arange(half_width, dtype=jnp.float32) * (-2.0 * math.log(10000.0) / inputs.shape[-1]))
    angles = spots.astype(jnp.float32)[:, None] * frequency[None, :]
    cos_part = jnp.cos(angles)
    sin_part = jnp.sin(angles) * direction
    if inputs.ndim == 3:
        cos_part = cos_part[:, None, :]
        sin_part = sin_part[:, None, :]
    first_half = inputs[..., :half_width]
    second_half = inputs[..., half_width:]
    return jnp.concatenate([first_half * cos_part - second_half * sin_part, second_half * cos_part + first_half * sin_part], axis=-1)

def merged(base, left_factor, right_factor):
    return low(base + matmul(left_factor, right_factor))

def merged_pair(base, left_factor, right_factor):
    key_half = matmul(left_factor[:, :UPDATE_RANK], right_factor[:, :HEAD_SIZE])
    value_half = matmul(left_factor[:, UPDATE_RANK:], right_factor[:, HEAD_SIZE:])
    return low(base + jnp.concatenate([key_half, value_half], axis=1))

def attend(queries, key_rows, values, token_sequence_index, positions):
    total_rows = queries.shape[0]
    block_rows = math.gcd(total_rows, 512)
    block_count = total_rows // block_rows
    query_blocks = queries.reshape(block_count, block_rows, HQ, HEAD_SIZE)
    seq_blocks = token_sequence_index.reshape(block_count, block_rows)
    spot_blocks = positions.reshape(block_count, block_rows)

    def one_block(pieces):
        query_block, seq_block, spot_block = pieces
        scores = jnp.einsum('qhd,kd->hqk', query_block, key_rows, precision=precise) * HEAD_SIZE ** (-0.5)
        scores = low_back(scores)
        allowed = (seq_block[:, None] == token_sequence_index[None, :]) & (positions[None, :] <= spot_block[:, None])
        scores = jnp.where(allowed[None], scores, MASKED_SCORE)
        weights = low(jax.nn.softmax(scores, axis=-1))
        return jnp.einsum('hqk,kd->qhd', weights, values, precision=precise)
    outputs = lax.map(jax.checkpoint(one_block), (query_blocks, seq_blocks, spot_blocks))
    return outputs.reshape(total_rows, HQ * HEAD_SIZE)

def block_layer(inputs, token_sequence_index, positions):
    tokens, attention_norm_gain, feedforward_norm_gain = (inputs[0], inputs[1], inputs[2])
    q_base, kv_base, o_base, gate_base, up_base, down_base = inputs[3:9]
    q_left, q_right, kv_left, kv_right, o_left, o_right = inputs[9:15]
    gate_left, gate_right, up_left, up_right, down_left, down_right = inputs[15:21]
    merged_q = merged(q_base, q_left, q_right)
    merged_kv = merged_pair(kv_base, kv_left, kv_right)
    merged_o = merged(o_base, o_left, o_right)
    merged_gate = merged(gate_base, gate_left, gate_right)
    merged_up = merged(up_base, up_left, up_right)
    merged_down = merged(down_base, down_left, down_right)
    normed = low(rms_norm(tokens, attention_norm_gain))
    queries = low_back(matmul(normed, merged_q))
    key_value = low_back(matmul(normed, merged_kv))
    queries = low(rotate(queries.reshape(-1, HQ, HEAD_SIZE), positions, 1.0))
    key_rows = low(rotate(key_value[:, :HEAD_SIZE], positions, 1.0))
    values = low(key_value[:, HEAD_SIZE:])
    attended = low(low_back(attend(queries, key_rows, values, token_sequence_index, positions)))
    branch = low_back(matmul(attended, merged_o.T))
    middle = tokens + branch
    normed2 = low(rms_norm(middle, feedforward_norm_gain))
    gate_act = low_back(matmul(normed2, merged_gate))
    up_act = low_back(matmul(normed2, merged_up))
    hidden = low(jax.nn.gelu(gate_act, approximate=True) * up_act)
    return middle + low_back(matmul(hidden, merged_down.T))

def reference(tokens, cotangent, token_sequence_index, positions, token_exit_loop, current_loop, attention_norm_gain, feedforward_norm_gain, probe, query_matrix, key_value_matrix, output_matrix, gate_matrix, up_matrix, down_matrix, query_update_left, query_update_right, key_value_update_left, key_value_update_right, output_update_left, output_update_right, gate_update_left, gate_update_right, up_update_left, up_update_right, down_update_left, down_update_right):
    loop_selection = current_loop[0]
    update_tables = (query_update_left, query_update_right, key_value_update_left, key_value_update_right, output_update_left, output_update_right, gate_update_left, gate_update_right, up_update_left, up_update_right, down_update_left, down_update_right)
    selected_factor = [lax.dynamic_index_in_dim(update_table, loop_selection, 0, keepdims=False).astype(jnp.float32) for update_table in update_tables]
    base_list = [weight.astype(jnp.float32) for weight in (query_matrix, key_value_matrix, output_matrix, gate_matrix, up_matrix, down_matrix)]
    primals = [tokens.astype(jnp.float32), attention_norm_gain, feedforward_norm_gain] + base_list + selected_factor

    def run_layer(*inputs):
        output_rows = block_layer(inputs, token_sequence_index, positions)
        confidence = jnp.mean(jax.nn.sigmoid(matmul(output_rows, probe))).reshape(1)
        return (output_rows, confidence)
    output_rows, pullback, confidence = jax.vjp(run_layer, *primals, has_aux=True)
    gradients = pullback(cotangent.astype(jnp.float32))
    levels = jnp.arange(LOOP_COUNT, dtype=jnp.int32)
    counts = lax.optimization_barrier(jnp.sum((token_exit_loop[:, None] == levels[None, :]).astype(jnp.int32), axis=0))

    def place_loop(grad_item):
        return jnp.zeros((LOOP_COUNT,) + grad_item.shape, jnp.float32).at[loop_selection].set(grad_item)
    return (counts, confidence, output_rows.astype(jnp.bfloat16), gradients[0], gradients[1], gradients[2], gradients[3], gradients[4], gradients[5], gradients[6], gradients[7], gradients[8], place_loop(gradients[9]), place_loop(gradients[10]), place_loop(gradients[11]), place_loop(gradients[12]), place_loop(gradients[13]), place_loop(gradients[14]), place_loop(gradients[15]), place_loop(gradients[16]), place_loop(gradients[17]), place_loop(gradients[18]), place_loop(gradients[19]), place_loop(gradients[20]))
```

```python
import math

import jax
import jax.numpy as jnp
from jax import lax
from jax.sharding import PartitionSpec as P

HEAD_SIZE = 256
LOOP_COUNT = 3


EPSILON = 1e-06
MASKED_SCORE = -1e30
precise = lax.Precision.HIGHEST
f32 = jnp.float32
bf16 = jnp.bfloat16


def rms_norm(inputs, gain):
    return inputs * lax.rsqrt(jnp.mean(inputs * inputs, axis=-1, keepdims=True) + EPSILON) * gain


def rotate(inputs, spots, direction):
    half_width = inputs.shape[-1] // 2
    frequency = jnp.exp(
        jnp.arange(half_width, dtype=jnp.float32) * (-2.0 * math.log(10000.0) / inputs.shape[-1])
    )
    angles = spots.astype(jnp.float32)[:, None] * frequency[None, :]
    cos_part = jnp.cos(angles)
    sin_part = jnp.sin(angles) * direction
    if inputs.ndim == 3:
        cos_part = cos_part[:, None, :]
        sin_part = sin_part[:, None, :]
    first_half = inputs[..., :half_width]
    second_half = inputs[..., half_width:]
    return jnp.concatenate(
        [
            first_half * cos_part - second_half * sin_part,
            second_half * cos_part + first_half * sin_part,
        ],
        axis=-1,
    )


def update_delta(left_factor, right_factor, factor_pairs):
    if factor_pairs:
        rank_half = left_factor.shape[1] // 2
        width_half = right_factor.shape[1] // 2
        key_half = jnp.dot(
            left_factor[:, :rank_half],
            right_factor[:, :width_half],
            preferred_element_type=jnp.float32,
        )
        value_half = jnp.dot(
            left_factor[:, rank_half:],
            right_factor[:, width_half:],
            preferred_element_type=jnp.float32,
        )
        return jnp.concatenate([key_half, value_half], axis=1)
    return jnp.dot(left_factor, right_factor, preferred_element_type=jnp.float32)


def attention_weights(queries, key_rows, query_seq, query_spots, key_seq, key_spots, score_scale):
    scores = (
        jnp.einsum("qhd,kd->hqk", queries, key_rows, preferred_element_type=jnp.float32)
        * score_scale
    )
    allowed = (query_seq[:, None] == key_seq[None, :]) & (
        key_spots[None, :] <= query_spots[:, None]
    )
    scores = jnp.where(allowed[None], scores, MASKED_SCORE)
    return jax.nn.softmax(scores, axis=-1)


def gated_unit(gate_act, up_act):
    return jax.nn.gelu(gate_act, approximate=True) * up_act


def dot(left, right):
    return jnp.dot(left, right, preferred_element_type=f32)


def dot_rows(left, right):
    return lax.dot_general(left, right, (((0,), (0,)), ((), ())), preferred_element_type=f32)


def dot_cols(left, right):
    return lax.dot_general(left, right, (((1,), (1,)), ((), ())), preferred_element_type=f32)


def swap(value, axis, bit):
    count = lax.axis_size(axis)
    return lax.ppermute(value, axis, [(place, place ^ bit) for place in range(count)])


def far_bits():
    bit = lax.axis_size("dp") // 2
    bits = []
    while bit > 1:
        bits.append(bit)
        bit = bit // 2
    return bits


def grow(value, axis, bit):
    return jnp.concatenate([value, swap(value, axis, bit)], axis=0)


def fold(value, axis, bit):
    half = value.shape[0] // 2
    arrived = swap(value[half:].astype(bf16), axis, bit)
    return value[:half] + arrived.astype(f32)


def gather_mp(value):
    return grow(grow(value, "mp", 2), "mp", 1)


def scatter_mp(value):
    return fold(fold(value, "mp", 1), "mp", 2)


def gather_all(value):
    for bit in far_bits():
        value = grow(value, "dp", bit)
    half = value.shape[0] // 2
    front = grow(grow(value[:half], "dp", 1), "mp", 2)
    rear = grow(grow(value[half:], "mp", 2), "dp", 1)
    return grow(jnp.concatenate([front, rear], axis=0), "mp", 1)


def scatter_all(value):
    value = fold(value, "mp", 1)
    half = value.shape[0] // 2
    front = fold(fold(value[:half], "mp", 2), "dp", 1)
    rear = fold(fold(value[half:], "dp", 1), "mp", 2)
    value = jnp.concatenate([front, rear], axis=0)
    for bit in reversed(far_bits()):
        value = fold(value, "dp", bit)
    return value


def sum_all(value):
    for axis in ("mp", "dp"):
        bit = 1
        while bit < lax.axis_size(axis):
            value = value + swap(value, axis, bit)
            bit = bit * 2
    return value


def sum_mp(value):
    value = value + swap(value, "mp", 1)
    low = value.astype(bf16)
    return low.astype(f32) + swap(low, "mp", 2).astype(f32)


def exchange_dp(block_for):
    count = lax.axis_size("dp")
    me = lax.axis_index("dp")
    own = block_for(me)
    result = jnp.zeros((count,) + own.shape, own.dtype)
    result = lax.dynamic_update_index_in_dim(result, own, me, 0)
    for step in range(count - 1, 0, -1):
        place = jnp.bitwise_xor(me, step)
        arrived = swap(block_for(place), "dp", step)
        result = lax.dynamic_update_index_in_dim(result, arrived, place, 0)
    return result


def relative_rows(value):
    me = lax.axis_index("mp")
    rows = value.shape[0] // 4
    return jnp.concatenate(
        [
            lax.dynamic_slice_in_dim(value, jnp.bitwise_xor(me, step) * rows, rows, 0)
            for step in (0, 2, 1, 3)
        ],
        axis=0,
    )


def natural_rows(value):
    me = lax.axis_index("mp")
    rows = value.shape[0] // 4
    blocks = []
    for place in range(4):
        step = jnp.bitwise_xor(me, place)
        slot = (step & 1) * 2 + (step >> 1)
        blocks.append(lax.dynamic_slice_in_dim(value, slot * rows, rows, 0))
    return jnp.concatenate(blocks, axis=0)


def body(
    tokens,
    cotangent,
    token_sequence_index,
    positions,
    token_exit_loop,
    current_loop,
    attention_norm_gain,
    feedforward_norm_gain,
    probe,
    query_matrix,
    key_value_matrix,
    output_matrix,
    gate_matrix,
    up_matrix,
    down_matrix,
    query_update_left,
    query_update_right,
    key_value_update_left,
    key_value_update_right,
    output_update_left,
    output_update_right,
    gate_update_left,
    gate_update_right,
    up_update_left,
    up_update_right,
    down_update_left,
    down_update_right,
):
    loop_selection = current_loop[0]
    score_scale = HEAD_SIZE ** (-0.5)
    mp_count = lax.axis_size("mp")
    dp_count = lax.axis_size("dp")
    mp_place = lax.axis_index("mp")
    dp_place = lax.axis_index("dp")
    row_count, model_width = tokens.shape
    own_rows = row_count // mp_count
    head_count = query_matrix.shape[1] // HEAD_SIZE
    hidden_own = gate_matrix.shape[1] // dp_count
    query_cols = query_matrix.shape[1]
    block_width = query_matrix.shape[0]

    def pick(table):
        return lax.dynamic_index_in_dim(table, loop_selection, 0, keepdims=False)

    q_left, kv_left, o_left = map(
        pick, (query_update_left, key_value_update_left, output_update_left)
    )
    gate_left, up_left, down_left = map(pick, (gate_update_left, up_update_left, down_update_left))
    q_right, kv_right, o_right = map(
        pick, (query_update_right, key_value_update_right, output_update_right)
    )
    gate_right, up_right, down_right = map(
        pick, (gate_update_right, up_update_right, down_update_right)
    )

    def merge(base, left, right, pairs=False):
        return (base.astype(f32) + update_delta(left, right, pairs)).astype(bf16)

    def own_slice(value):
        return lax.dynamic_slice_in_dim(value, mp_place * own_rows, own_rows, 0)

    block_rows = block_width // mp_count
    kv_base_own = lax.dynamic_slice_in_dim(key_value_matrix, mp_place * block_rows, block_rows, 0)
    kv_left_own = lax.dynamic_slice_in_dim(kv_left, mp_place * block_rows, block_rows, 0)
    kv_full = lax.all_gather(
        merge(kv_base_own, kv_left_own, kv_right, True), ("dp", "mp"), axis=0, tiled=True
    )
    q_full = lax.all_gather(merge(query_matrix, q_left, q_right), "dp", axis=0, tiled=True)
    o_full = lax.all_gather(merge(output_matrix, o_left, o_right), "dp", axis=0, tiled=True)

    def spread(shard):
        shape = (dp_count * shard.shape[0], hidden_own)
        return exchange_dp(
            lambda place: lax.dynamic_slice_in_dim(shard, place * hidden_own, hidden_own, 1)
        ).reshape(shape)

    gate_own = spread(merge(gate_matrix, gate_left, gate_right))
    up_own = spread(merge(up_matrix, up_left, up_right))
    down_own = spread(merge(down_matrix, down_left, down_right))
    gate_up_own = jnp.concatenate([gate_own, up_own], axis=1)
    left_block = jnp.concatenate([gate_left, up_left, down_left], axis=1)
    left_all = lax.all_gather(
        lax.dynamic_slice_in_dim(left_block, mp_place * block_rows, block_rows, 0),
        ("dp", "mp"),
        axis=0,
        tiled=True,
    )
    cotangent_own = own_slice(cotangent)
    cotangent_all = gather_all(cotangent_own)

    tokens_wide = relative_rows(tokens).astype(f32)
    query_seq = relative_rows(token_sequence_index)
    query_spots = relative_rows(positions)
    normed_b = rms_norm(tokens_wide, attention_norm_gain).astype(bf16)
    pair_own = dot(normed_b[:own_rows], kv_full)
    spots_own = query_spots[:own_rows]
    outgoing = jnp.concatenate(
        [rotate(pair_own[:, :HEAD_SIZE], spots_own, 1.0), pair_own[:, HEAD_SIZE:]], axis=1
    ).astype(bf16)
    all_pairs = gather_all(outgoing)
    all_places = gather_all(jnp.stack([query_seq[:own_rows], spots_own], axis=1))
    all_seq = all_places[:, 0]
    all_spots = all_places[:, 1]
    all_keys = all_pairs[:, :HEAD_SIZE]
    all_values = all_pairs[:, HEAD_SIZE:]
    queries = dot(normed_b, q_full)
    query_b = rotate(queries.reshape(row_count, head_count, HEAD_SIZE), query_spots, 1.0).astype(
        bf16
    )
    weights_soft = attention_weights(
        query_b, all_keys, query_seq, query_spots, all_seq, all_spots, score_scale
    )
    weights_low = weights_soft.astype(bf16)
    attended = jnp.einsum("hqk,kd->qhd", weights_low, all_values, preferred_element_type=f32)
    attended_b = attended.reshape(row_count, query_cols).astype(bf16)
    branch_own = scatter_mp(dot_cols(attended_b, o_full))
    middle = tokens_wide[:own_rows] + branch_own
    normed2_b = rms_norm(middle, feedforward_norm_gain).astype(bf16)

    normed2_all = gather_all(normed2_b)
    gate_up = dot(normed2_all, gate_up_own)
    gate_act = gate_up[:, :hidden_own]
    up_act = gate_up[:, hidden_own:]
    hidden_grad = dot(cotangent_all, down_own)
    hidden_value, unit_pull = jax.vjp(gated_unit, gate_act, up_act)
    hidden_b = hidden_value.astype(bf16)
    gate_grad, up_grad = unit_pull(hidden_grad)
    unit_grad_b = jnp.concatenate([gate_grad.astype(bf16), up_grad.astype(bf16)], axis=1)
    normed2_grad = scatter_all(dot_cols(unit_grad_b, gate_up_own))
    mlp_branch = scatter_all(dot_cols(hidden_b, down_own))

    output_rows = middle + mlp_branch
    mixed = natural_rows(gather_mp(output_rows.astype(bf16)))
    confidence_own = jnp.sum(jax.nn.sigmoid(jnp.dot(output_rows, probe, precision=precise)))
    levels = jnp.arange(LOOP_COUNT, dtype=jnp.int32)
    exit_own = own_slice(token_exit_loop)
    depth_own = jnp.sum((exit_own[:, None] == levels[None, :]).astype(f32), axis=0)

    gate_up_grad = dot_rows(normed2_all, unit_grad_b)
    down_grad = dot_rows(cotangent_all, hidden_b)
    rank = gate_left.shape[1]
    rank_own = rank // dp_count

    def collect(grad_cols, left_cols):
        grad_b = grad_cols.astype(bf16)
        right_part = dot_rows(left_cols, grad_b).astype(bf16)
        blocks = jnp.concatenate(
            [
                grad_b.reshape(dp_count, block_width, hidden_own),
                right_part.reshape(dp_count, rank_own, hidden_own),
            ],
            axis=1,
        )
        arrived = exchange_dp(
            lambda place: lax.dynamic_index_in_dim(blocks, place, 0, keepdims=False)
        )
        rows = jnp.swapaxes(arrived, 0, 1).reshape(block_width + rank_own, dp_count * hidden_own)
        return rows[:block_width], rows[block_width:].astype(f32)

    down_weight_b, down_lora_b = collect(down_grad, left_all[:, 2 * rank :])
    gate_weight_b, gate_lora_b = collect(gate_up_grad[:, :hidden_own], left_all[:, :rank])
    up_weight_b, up_lora_b = collect(gate_up_grad[:, hidden_own:], left_all[:, rank : 2 * rank])
    mlp_lora_a = sum_mp(
        jnp.concatenate(
            [
                dot_cols(gate_weight_b, gate_right),
                dot_cols(up_weight_b, up_right),
                dot_cols(down_weight_b, down_right),
            ],
            axis=1,
        )
    )

    unused_norm, mlp_pull = jax.vjp(rms_norm, middle, feedforward_norm_gain)
    middle_norm_grad, mlp_gain_part = mlp_pull(normed2_grad)
    middle_grad = cotangent_own.astype(f32) + middle_norm_grad
    branch_grad_own = middle_grad.astype(bf16)
    branch_grad = gather_mp(branch_grad_own)
    attended_grad_b = (
        dot(branch_grad, o_full).astype(bf16).reshape(row_count, head_count, HEAD_SIZE)
    )
    prob_grad = jnp.einsum("qhd,kd->hqk", attended_grad_b, all_values, preferred_element_type=f32)
    score_grad_b = (
        weights_soft * (prob_grad - jnp.sum(prob_grad * weights_soft, axis=-1, keepdims=True))
    ).astype(bf16)
    keys_grad = (
        jnp.einsum("hqk,qhd->kd", score_grad_b, query_b, preferred_element_type=f32) * score_scale
    )
    values_grad = jnp.einsum(
        "hqk,qhd->kd", weights_low, attended_grad_b, preferred_element_type=f32
    )
    pair_grad_own = scatter_all(jnp.concatenate([keys_grad, values_grad], axis=1))
    pair_grad_b = jnp.concatenate(
        [rotate(pair_grad_own[:, :HEAD_SIZE], spots_own, -1.0), pair_grad_own[:, HEAD_SIZE:]],
        axis=1,
    ).astype(bf16)
    query_grad = (
        jnp.einsum("hqk,kd->qhd", score_grad_b, all_keys, preferred_element_type=f32) * score_scale
    )
    query_grad_b = (
        rotate(query_grad, query_spots, -1.0).reshape(row_count, query_cols).astype(bf16)
    )
    normed_grad = scatter_mp(dot_cols(query_grad_b, q_full)) + dot_cols(pair_grad_b, kv_full)
    unused_first, attn_pull = jax.vjp(rms_norm, tokens_wide[:own_rows], attention_norm_gain)
    inputs_norm_grad, attn_gain_part = attn_pull(normed_grad)
    tokens_grad = natural_rows(gather_mp(middle_grad + inputs_norm_grad))

    def all_token_cols(rows_own):
        arrived = exchange_dp(
            lambda place: lax.dynamic_slice_in_dim(rows_own, place * block_width, block_width, 1)
        )
        arrived = gather_mp(arrived.reshape(dp_count * own_rows, block_width))
        arrived = arrived.reshape(mp_count, dp_count, own_rows, block_width)
        return jnp.swapaxes(arrived, 0, 1).reshape(dp_count * row_count, block_width)

    normed_cols = all_token_cols(normed_b[:own_rows])
    branch_cols = all_token_cols(branch_grad_own)
    attended_all = lax.all_gather(attended_b, "dp", axis=0, tiled=True)
    query_grad_all = lax.all_gather(query_grad_b, "dp", axis=0, tiled=True)
    pair_grad_all = lax.all_gather(pair_grad_b, "dp", axis=0, tiled=True)
    pair_grad_all = gather_mp(pair_grad_all).reshape(mp_count, dp_count, own_rows, -1)
    pair_grad_all = jnp.swapaxes(pair_grad_all, 0, 1).reshape(dp_count * row_count, -1)
    q_weight_grad = dot_rows(normed_cols, query_grad_all)
    kv_weight_grad = dot_rows(normed_cols, pair_grad_all)
    o_weight_grad = dot_rows(branch_cols, attended_all)
    q_weight_b = q_weight_grad.astype(bf16)
    kv_weight_b = kv_weight_grad.astype(bf16)
    o_weight_b = o_weight_grad.astype(bf16)
    qo_lora_a = sum_mp(
        jnp.concatenate([dot_cols(q_weight_b, q_right), dot_cols(o_weight_b, o_right)], axis=1)
    )
    kv_lora_a = jnp.concatenate(
        [
            dot_cols(kv_weight_b[:, :HEAD_SIZE], kv_right[:, :HEAD_SIZE]),
            dot_cols(kv_weight_b[:, HEAD_SIZE:], kv_right[:, HEAD_SIZE:]),
        ],
        axis=1,
    )
    right_parts = jnp.concatenate(
        [
            dot_rows(q_left, q_weight_b),
            dot_rows(o_left, o_weight_b),
            dot_rows(kv_left[:, :rank], kv_weight_b[:, :HEAD_SIZE]),
            dot_rows(kv_left[:, rank:], kv_weight_b[:, HEAD_SIZE:]),
        ],
        axis=1,
    ).astype(bf16)
    right_grads = jnp.sum(
        exchange_dp(
            lambda place: lax.dynamic_slice_in_dim(right_parts, place * rank_own, rank_own, 0)
        ).astype(f32),
        axis=0,
    )

    small = sum_all(
        jnp.concatenate([attn_gain_part, mlp_gain_part, depth_own, confidence_own.reshape(1)])
    )
    gain_width = model_width // dp_count
    attn_gain_grad = lax.dynamic_slice_in_dim(small, dp_place * gain_width, gain_width, 0)
    mlp_gain_grad = lax.dynamic_slice_in_dim(
        small, model_width + dp_place * gain_width, gain_width, 0
    )
    counts = small[2 * model_width : 2 * model_width + LOOP_COUNT].astype(jnp.int32)
    confidence = small[2 * model_width + LOOP_COUNT :] / (row_count * dp_count)

    def place_loop(grad_item):
        empty = jnp.zeros((LOOP_COUNT,) + grad_item.shape, f32)
        return lax.dynamic_update_index_in_dim(empty, grad_item, loop_selection, 0)

    return (
        counts,
        confidence,
        mixed,
        tokens_grad,
        attn_gain_grad,
        mlp_gain_grad,
        q_weight_grad,
        kv_weight_grad,
        o_weight_grad,
        gate_weight_b.astype(f32),
        up_weight_b.astype(f32),
        down_weight_b.astype(f32),
        place_loop(qo_lora_a[:, :rank]),
        place_loop(right_grads[:, :query_cols]),
        place_loop(kv_lora_a),
        place_loop(right_grads[:, 2 * query_cols :]),
        place_loop(qo_lora_a[:, rank:]),
        place_loop(right_grads[:, query_cols : 2 * query_cols]),
        place_loop(mlp_lora_a[:, :rank]),
        place_loop(gate_lora_b),
        place_loop(mlp_lora_a[:, rank : 2 * rank]),
        place_loop(up_lora_b),
        place_loop(mlp_lora_a[:, 2 * rank :]),
        place_loop(down_lora_b),
    )


def solution(mesh):
    return jax.shard_map(
        body,
        mesh=mesh,
        in_specs=(
            P("dp", None),
            P("dp", None),
            P("dp"),
            P("dp"),
            P("dp"),
            P(),
            P(),
            P(),
            P(),
            P("dp", "mp"),
            P("dp", None),
            P("dp", "mp"),
            P("dp", "mp"),
            P("dp", "mp"),
            P("dp", "mp"),
            P(None, "dp", None),
            P(None, None, "mp"),
            P(None, "dp", None),
            P(),
            P(None, "dp", None),
            P(None, None, "mp"),
            P(None, "dp", None),
            P(None, None, "mp"),
            P(None, "dp", None),
            P(None, None, "mp"),
            P(None, "dp", None),
            P(None, None, "mp"),
        ),
        out_specs=(
            P(),
            P(),
            P("dp", None),
            P("dp", None),
            P("dp"),
            P("dp"),
            P("dp", "mp"),
            P("dp", None),
            P("dp", "mp"),
            P("dp", "mp"),
            P("dp", "mp"),
            P("dp", "mp"),
            P(None, "dp", None),
            P(None, "dp", "mp"),
            P(None, "dp", None),
            P(None, "dp", None),
            P(None, "dp", None),
            P(None, "dp", "mp"),
            P(None, "dp", None),
            P(None, "dp", "mp"),
            P(None, "dp", None),
            P(None, "dp", "mp"),
            P(None, "dp", None),
            P(None, "dp", "mp"),
        ),
        check_vma=False,
    )
```

```python
import math

import jax
import jax.numpy as jnp
from jax import lax
from jax.experimental import pallas as pl
from jax.experimental.pallas import tpu as pltpu
from jax.sharding import PartitionSpec as P

HEAD_SIZE = 256
LOOP_COUNT = 3


EPSILON = 1e-06
MASKED_SCORE = -1e30
precise = lax.Precision.HIGHEST
f32 = jnp.float32
bf16 = jnp.bfloat16


def rms_norm(inputs, gain):
    return inputs * lax.rsqrt(jnp.mean(inputs * inputs, axis=-1, keepdims=True) + EPSILON) * gain


def rotate(inputs, spots, direction):
    half_width = inputs.shape[-1] // 2
    frequency = jnp.exp(
        jnp.arange(half_width, dtype=jnp.float32) * (-2.0 * math.log(10000.0) / inputs.shape[-1])
    )
    angles = spots.astype(jnp.float32)[:, None] * frequency[None, :]
    cos_part = jnp.cos(angles)
    sin_part = jnp.sin(angles) * direction
    if inputs.ndim == 3:
        cos_part = cos_part[:, None, :]
        sin_part = sin_part[:, None, :]
    first_half = inputs[..., :half_width]
    second_half = inputs[..., half_width:]
    return jnp.concatenate(
        [
            first_half * cos_part - second_half * sin_part,
            second_half * cos_part + first_half * sin_part,
        ],
        axis=-1,
    )


def update_delta(left_factor, right_factor, factor_pairs):
    if factor_pairs:
        rank_half = left_factor.shape[1] // 2
        width_half = right_factor.shape[1] // 2
        key_half = jnp.dot(
            left_factor[:, :rank_half],
            right_factor[:, :width_half],
            preferred_element_type=jnp.float32,
        )
        value_half = jnp.dot(
            left_factor[:, rank_half:],
            right_factor[:, width_half:],
            preferred_element_type=jnp.float32,
        )
        return jnp.concatenate([key_half, value_half], axis=1)
    return jnp.dot(left_factor, right_factor, preferred_element_type=jnp.float32)


def attention_weights(queries, key_rows, query_seq, query_spots, key_seq, key_spots, score_scale):
    scores = (
        jnp.einsum("qhd,kd->hqk", queries, key_rows, preferred_element_type=jnp.float32)
        * score_scale
    )
    allowed = (query_seq[:, None] == key_seq[None, :]) & (
        key_spots[None, :] <= query_spots[:, None]
    )
    scores = jnp.where(allowed[None], scores, MASKED_SCORE)
    return jax.nn.softmax(scores, axis=-1)


def dot(left, right):
    return jnp.dot(left, right, preferred_element_type=f32)


def dot_rows(left, right):
    return lax.dot_general(left, right, (((0,), (0,)), ((), ())), preferred_element_type=f32)


def dot_cols(left, right):
    return lax.dot_general(left, right, (((1,), (1,)), ((), ())), preferred_element_type=f32)


def swap(value, axis, bit):
    count = lax.axis_size(axis)
    return lax.ppermute(value, axis, [(place, place ^ bit) for place in range(count)])


def exchange(blocks):
    return lax.all_to_all(blocks, "dp", 0, 0, tiled=True)


def far_bits():
    bit = lax.axis_size("dp") // 2
    bits = []
    while bit > 1:
        bits.append(bit)
        bit = bit // 2
    return bits


def grow(value, axis, bit):
    return jnp.concatenate([value, swap(value, axis, bit)], axis=0)


def fold(value, axis, bit):
    half = value.shape[0] // 2
    arrived = swap(value[half:].astype(bf16), axis, bit)
    return value[:half] + arrived.astype(f32)


def after(value, *others):
    total = jnp.zeros((), f32)
    for other in others:
        last = other[tuple(size - 1 for size in other.shape)]
        total = jnp.maximum(total, jnp.abs(last.astype(f32)))
    return value + jnp.minimum(total, 0.0).astype(value.dtype)


def halves(value):
    half = value.shape[0] // 2
    return value[:half], value[half:]


def gather_mp(value):
    place = lax.axis_index("mp")
    arrived = swap(value, "mp", 2)
    value = jnp.where(
        place < 2, jnp.stack([value, arrived], axis=0), jnp.stack([arrived, value], axis=0)
    )
    arrived = swap(value, "mp", 1)
    return jnp.where(
        place % 2 == 0, jnp.stack([value, arrived], axis=1), jnp.stack([arrived, value], axis=1)
    )


def scatter_mp(value):
    place = lax.axis_index("mp")
    for axis, bit, own in ((1, 1, place % 2), (0, 2, place // 2)):
        if axis == 1:
            value = value.reshape((2, 2, value.shape[0] // 4) + value.shape[1:])
        sent = lax.dynamic_index_in_dim(value, 1 - own, axis, keepdims=False)
        kept = lax.dynamic_index_in_dim(value, own, axis, keepdims=False)
        value = kept + swap(sent.astype(bf16), "mp", bit).astype(f32)
    return value


def gather_far(value):
    for bit in far_bits():
        value = grow(value, "dp", bit)
    return value


def gather_near(value):
    half = value.shape[0] // 2
    front = grow(grow(value[:half], "dp", 1), "mp", 2)
    rear = grow(grow(value[half:], "mp", 2), "dp", 1)
    return jnp.concatenate([front, rear], axis=0)


def other_core(value):
    return swap(value, "mp", 1)


def scatter_near(sent, kept):
    value = kept + swap(sent.astype(bf16), "mp", 1).astype(f32)
    half = value.shape[0] // 2
    front = fold(fold(value[:half], "mp", 2), "dp", 1)
    rear = fold(fold(value[half:], "dp", 1), "mp", 2)
    return jnp.concatenate([front, rear], axis=0)


def scatter_far(value):
    for bit in reversed(far_bits()):
        value = fold(value, "dp", bit)
    return value


def sum_all(value):
    for axis in ("mp", "dp"):
        bit = 1
        while bit < lax.axis_size(axis):
            value = value + swap(value, axis, bit)
            bit = bit * 2
    return value


def sum_mp(value):
    value = value + swap(value, "mp", 1)
    low = value.astype(bf16)
    return low.astype(f32) + swap(low, "mp", 2).astype(f32)


def merge_kernel(loop_ref, *refs):
    out_ref = refs[-1]
    width = refs[0].shape[1]
    for index in range(len(refs) // 3):
        base_ref, left_ref, right_ref = refs[3 * index : 3 * index + 3]
        delta = jnp.dot(left_ref[0], right_ref[0], preferred_element_type=f32)
        merged = base_ref[...].astype(f32) + delta
        out_ref[0, :, index * width : (index + 1) * width] = merged.astype(bf16)


def merge_blocks(loop, places, weights):
    rows, columns = weights[0][0].shape
    rank = weights[0][1].shape[2]
    width = columns // places
    specs = []
    arrays = []
    for base, left, right in weights:
        specs.append(pl.BlockSpec((rows, width), lambda place, loop_ref: (0, place)))
        specs.append(pl.BlockSpec((1, rows, rank), lambda place, loop_ref: (loop_ref[0], 0, 0)))
        specs.append(
            pl.BlockSpec((1, rank, width), lambda place, loop_ref: (loop_ref[0], 0, place))
        )
        arrays += [base, left, right]
    return pl.pallas_call(
        merge_kernel,
        out_shape=jax.ShapeDtypeStruct((places, rows, width * len(weights)), bf16),
        grid_spec=pltpu.PrefetchScalarGridSpec(
            num_scalar_prefetch=1,
            grid=(places,),
            in_specs=specs,
            out_specs=pl.BlockSpec(
                (1, rows, width * len(weights)), lambda place, loop_ref: (place, 0, 0)
            ),
        ),
        compiler_params=pltpu.CompilerParams(vmem_limit_bytes=48 * 2**20),
    )(loop, *arrays)


def receive_kernel(loop_ref, arrived_ref, right_ref, grad_ref, left_grad_ref):
    rows = grad_ref.shape[0]
    block = arrived_ref[0][:rows]
    grad_ref[...] = block.astype(f32)
    part = lax.dot_general(
        block, right_ref[0], (((1,), (1,)), ((), ())), preferred_element_type=f32
    )

    @pl.when(pl.program_id(0) == 0)
    def first():
        left_grad_ref[...] = part

    @pl.when(pl.program_id(0) > 0)
    def later():
        left_grad_ref[...] += part


def receive_grad(loop, arrived, right, rows):
    places, all_rows, width = arrived.shape
    rank = right.shape[1]
    return pl.pallas_call(
        receive_kernel,
        out_shape=(
            jax.ShapeDtypeStruct((rows, places * width), f32),
            jax.ShapeDtypeStruct((rows, rank), f32),
        ),
        grid_spec=pltpu.PrefetchScalarGridSpec(
            num_scalar_prefetch=1,
            grid=(places,),
            in_specs=[
                pl.BlockSpec((1, all_rows, width), lambda place, loop_ref: (place, 0, 0)),
                pl.BlockSpec((1, rank, width), lambda place, loop_ref: (loop_ref[0], 0, place)),
            ],
            out_specs=(
                pl.BlockSpec((rows, width), lambda place, loop_ref: (0, place)),
                pl.BlockSpec((rows, rank), lambda place, loop_ref: (0, 0)),
            ),
        ),
        compiler_params=pltpu.CompilerParams(vmem_limit_bytes=48 * 2**20),
    )(loop, arrived, right)


def feed_kernel(
    normed_ref, cotangent_ref, gate_down_ref, up_ref, hidden_ref, grads_ref, partial_ref
):
    width = up_ref.shape[1]
    normed = normed_ref[...]
    gate_act = jnp.dot(normed, gate_down_ref[:, :width], preferred_element_type=f32)
    up_act = jnp.dot(normed, up_ref[...], preferred_element_type=f32)
    hidden_grad = jnp.dot(
        cotangent_ref[...], gate_down_ref[:, width:], preferred_element_type=f32
    )
    scale = math.sqrt(2.0 / math.pi)
    square = gate_act * gate_act
    tanh_part = jnp.tanh(scale * (gate_act + 0.044715 * (gate_act * square)))
    half_sum = 0.5 * (1.0 + tanh_part)
    gelu = gate_act * half_sum
    slope = half_sum + (0.5 * gate_act) * (1.0 - tanh_part * tanh_part) * (
        scale * (1.0 + (3.0 * 0.044715) * square)
    )
    hidden_ref[...] = (gelu * up_act).astype(bf16)
    gate_grad = (hidden_grad * up_act * slope).astype(bf16)
    up_grad = (hidden_grad * gelu).astype(bf16)
    grads_ref[:, :width] = gate_grad
    grads_ref[:, width:] = up_grad
    partial = lax.dot_general(
        gate_grad,
        gate_down_ref[:, :width],
        (((1,), (1,)), ((), ())),
        preferred_element_type=f32,
    ) + lax.dot_general(
        up_grad, up_ref[...], (((1,), (1,)), ((), ())), preferred_element_type=f32
    )
    partial_ref[...] = partial.astype(partial_ref.dtype)


def feed_forward(normed, cotangent, gate_down, up, kind):
    rows, model_width = normed.shape
    width = up.shape[1]
    tile = math.gcd(rows, 256)
    row_block = pl.BlockSpec((tile, model_width), lambda step: (step, 0))
    return pl.pallas_call(
        feed_kernel,
        out_shape=(
            jax.ShapeDtypeStruct((rows, width), bf16),
            jax.ShapeDtypeStruct((rows, 2 * width), bf16),
            jax.ShapeDtypeStruct((rows, model_width), kind),
        ),
        grid=(rows // tile,),
        in_specs=[
            row_block,
            row_block,
            pl.BlockSpec((model_width, 2 * width), lambda step: (0, 0)),
            pl.BlockSpec((model_width, width), lambda step: (0, 0)),
        ],
        out_specs=(
            pl.BlockSpec((tile, width), lambda step: (step, 0)),
            pl.BlockSpec((tile, 2 * width), lambda step: (step, 0)),
            row_block,
        ),
        compiler_params=pltpu.CompilerParams(vmem_limit_bytes=56 * 2**20),
    )(normed, cotangent, gate_down, up)


def body(
    tokens,
    cotangent,
    token_sequence_index,
    positions,
    token_exit_loop,
    current_loop,
    attention_norm_gain,
    feedforward_norm_gain,
    probe,
    query_matrix,
    key_value_matrix,
    output_matrix,
    gate_matrix,
    up_matrix,
    down_matrix,
    query_update_left,
    query_update_right,
    key_value_update_left,
    key_value_update_right,
    output_update_left,
    output_update_right,
    gate_update_left,
    gate_update_right,
    up_update_left,
    up_update_right,
    down_update_left,
    down_update_right,
):
    loop_selection = current_loop[0]
    score_scale = HEAD_SIZE ** (-0.5)
    mp_count = lax.axis_size("mp")
    dp_count = lax.axis_size("dp")
    mp_place = lax.axis_index("mp")
    dp_place = lax.axis_index("dp")
    row_count, model_width = tokens.shape
    own_rows = row_count // mp_count
    block_width, query_cols = query_matrix.shape
    head_count = query_cols // HEAD_SIZE
    hidden_own = gate_matrix.shape[1] // dp_count
    rank = gate_update_left.shape[2]
    rank_own = rank // dp_count

    def pick(table):
        return lax.dynamic_index_in_dim(table, loop_selection, 0, keepdims=False)

    q_left, kv_left, o_left = map(
        pick, (query_update_left, key_value_update_left, output_update_left)
    )
    gate_left, up_left, down_left = map(pick, (gate_update_left, up_update_left, down_update_left))
    q_right, kv_right, o_right = map(
        pick, (query_update_right, key_value_update_right, output_update_right)
    )
    def merge(base, left, right, pairs=False):
        return (base.astype(f32) + update_delta(left, right, pairs)).astype(bf16)

    def own_slice(value):
        return lax.dynamic_slice_in_dim(value, mp_place * own_rows, own_rows, 0)

    def to_places(shard, width):
        blocks = [shard[:, place * width : (place + 1) * width] for place in range(dp_count)]
        return jnp.stack(blocks, axis=0)

    block_rows = block_width // mp_count

    def block_slice(value):
        return lax.dynamic_slice_in_dim(value, mp_place * block_rows, block_rows, 0)

    kv_full = lax.all_gather(
        merge(block_slice(key_value_matrix), block_slice(kv_left), kv_right, True),
        ("dp", "mp"),
        axis=0,
        tiled=True,
    )
    q_o_full = lax.all_gather(
        jnp.concatenate(
            [merge(query_matrix, q_left, q_right), merge(output_matrix, o_left, o_right)], axis=1
        ),
        "dp",
        axis=0,
        tiled=True,
    )
    q_full = q_o_full[:, :query_cols]
    o_full = q_o_full[:, query_cols:]

    cotangent_own = own_slice(cotangent)
    cotangent_front = gather_near(gather_far(cotangent_own))
    cotangent_rear = other_core(cotangent_front)

    tokens_own = own_slice(tokens).astype(f32)
    normed_b = rms_norm(tokens.astype(f32), attention_norm_gain).astype(bf16)

    def all_token_cols(rows_own):
        cols = exchange(to_places(rows_own, block_width)).reshape(-1, block_width)
        cols = gather_mp(cols).reshape(mp_count, dp_count, own_rows, block_width)
        return jnp.swapaxes(cols, 0, 1).reshape(dp_count * row_count, block_width)

    normed_cols = all_token_cols(own_slice(normed_b))
    pair_own = dot(own_slice(normed_b), kv_full)
    seq_own = own_slice(token_sequence_index)
    spots_own = own_slice(positions)
    marks = jnp.stack([seq_own, spots_own // 64, spots_own % 64], axis=0).astype(bf16)
    marks = jnp.pad(marks, ((0, 5), (0, 2 * HEAD_SIZE - own_rows)))
    outgoing = jnp.concatenate(
        [
            rotate(pair_own[:, :HEAD_SIZE], spots_own, 1.0).astype(bf16),
            pair_own[:, HEAD_SIZE:].astype(bf16),
        ],
        axis=1,
    )
    outgoing = jnp.concatenate([outgoing, marks], axis=0)
    pairs_far = after(gather_far(outgoing), *halves(cotangent_front))
    pairs_front = gather_near(pairs_far)
    all_pairs = jnp.concatenate([pairs_front, other_core(pairs_front)], axis=0)
    all_pairs = all_pairs.reshape(-1, own_rows + 8, 2 * HEAD_SIZE)
    all_keys = all_pairs[:, :own_rows, :HEAD_SIZE].reshape(-1, HEAD_SIZE)
    all_values = all_pairs[:, :own_rows, HEAD_SIZE:].reshape(-1, HEAD_SIZE)
    all_marks = all_pairs[:, own_rows : own_rows + 3, :own_rows].astype(jnp.int32)
    all_seq = all_marks[:, 0].reshape(-1)
    all_spots = (all_marks[:, 1] * 64 + all_marks[:, 2]).reshape(-1)
    queries = dot(normed_b, q_full)
    query_b = rotate(queries.reshape(row_count, head_count, HEAD_SIZE), positions, 1.0).astype(
        bf16
    )
    gate_down = exchange(
        merge_blocks(
            after(current_loop, *halves(pairs_front)),
            dp_count,
            [
                (gate_matrix, gate_update_left, gate_update_right),
                (down_matrix, down_update_left, down_update_right),
            ],
        )
    ).reshape(model_width, 2 * hidden_own)
    query_b = after(query_b, normed_cols)
    weights_soft = attention_weights(
        query_b, all_keys, token_sequence_index, positions, all_seq, all_spots, score_scale
    )
    weights_low = weights_soft.astype(bf16)
    attended = jnp.einsum("hqk,kd->qhd", weights_low, all_values, preferred_element_type=f32)
    attended_b = attended.reshape(row_count, query_cols).astype(bf16)
    middle = tokens_own + scatter_mp(dot_cols(attended_b, o_full))
    normed2_b = rms_norm(middle, feedforward_norm_gain).astype(bf16)

    normed2_far = gather_far(after(normed2_b, gate_down))
    up_own = exchange(
        merge_blocks(
            after(current_loop, normed2_far),
            dp_count,
            [(up_matrix, up_update_left, up_update_right)],
        )
    ).reshape(model_width, hidden_own)
    normed2_front = gather_near(normed2_far)
    normed2_rear = other_core(after(normed2_front, up_own))
    left_block = jnp.concatenate([gate_left, up_left, down_left], axis=1)
    left_all = lax.all_gather(
        after(block_slice(left_block), gate_down), ("dp", "mp"), axis=0, tiled=True
    )

    hidden_front, grads_front, partial_front = feed_forward(
        normed2_front, cotangent_front, gate_down, up_own, f32
    )
    hidden_rear, grads_rear, partial_rear = feed_forward(
        normed2_rear, cotangent_rear, gate_down, up_own, bf16
    )
    normed2_near = scatter_near(partial_rear, partial_front)

    def weight_grad(front, rear, grads_front, grads_rear):
        return (dot_rows(front, grads_front) + dot_rows(rear, grads_rear)).astype(bf16)

    def to_blocks(grad_b, left_cols):
        right_part = dot_rows(left_cols, grad_b).astype(bf16)
        return [
            grad_b.reshape(dp_count, block_width, hidden_own),
            right_part.reshape(dp_count, rank_own, hidden_own),
        ]

    down_grad_b = weight_grad(cotangent_front, cotangent_rear, hidden_front, hidden_rear)
    gate_up_grad_b = weight_grad(normed2_front, normed2_rear, grads_front, grads_rear)
    down_gate_sent = exchange(
        jnp.concatenate(
            to_blocks(down_grad_b, left_all[:, 2 * rank :])
            + to_blocks(gate_up_grad_b[:, :hidden_own], left_all[:, :rank]),
            axis=1,
        )
    )
    up_grad_blocks = jnp.concatenate(
        to_blocks(gate_up_grad_b[:, hidden_own:], left_all[:, rank : 2 * rank]), axis=1
    )
    normed2_grad = scatter_far(after(normed2_near, down_gate_sent))

    hidden_late = after(jnp.zeros((1, hidden_own), bf16), *halves(normed2_near))
    down_own = gate_down[:, hidden_own:]
    mlp_branch = scatter_far(
        scatter_near(
            dot_cols(hidden_rear + hidden_late, down_own),
            dot_cols(hidden_front + hidden_late, down_own),
        )
    )
    output_rows = middle + mlp_branch
    mixed = gather_mp(output_rows.astype(bf16)).reshape(row_count, model_width)
    confidence_own = jnp.sum(jax.nn.sigmoid(jnp.dot(output_rows, probe, precision=precise)))
    levels = jnp.arange(LOOP_COUNT, dtype=jnp.int32)
    exit_own = own_slice(token_exit_loop)
    depth_own = jnp.sum((exit_own[:, None] == levels[None, :]).astype(f32), axis=0)

    unused_norm, mlp_pull = jax.vjp(rms_norm, middle, feedforward_norm_gain)
    middle_norm_grad, mlp_gain_part = mlp_pull(normed2_grad)
    middle_grad = cotangent_own.astype(f32) + middle_norm_grad
    branch_grad_own = middle_grad.astype(bf16)
    branch_grad = gather_mp(branch_grad_own).reshape(row_count, model_width)
    up_sent = exchange(after(up_grad_blocks, normed2_grad))
    attended_grad_b = (
        dot(branch_grad, o_full).astype(bf16).reshape(row_count, head_count, HEAD_SIZE)
    )
    prob_grad = jnp.einsum("qhd,kd->hqk", attended_grad_b, all_values, preferred_element_type=f32)
    score_grad_b = (
        weights_soft * (prob_grad - jnp.sum(prob_grad * weights_soft, axis=-1, keepdims=True))
    ).astype(bf16)
    keys_grad = (
        jnp.einsum("hqk,qhd->kd", score_grad_b, query_b, preferred_element_type=f32) * score_scale
    )
    values_grad = jnp.einsum(
        "hqk,qhd->kd", weights_low, attended_grad_b, preferred_element_type=f32
    )
    pair_partial = jnp.concatenate([keys_grad, values_grad], axis=1)
    half = pair_partial.shape[0] // 2
    pair_partial = after(pair_partial, up_sent)
    pair_near = scatter_near(pair_partial[half:], pair_partial[:half])
    o_partial = dot_rows(branch_grad, attended_b).astype(bf16)
    o_sent = exchange(after(o_partial.reshape(dp_count, block_width, query_cols), up_sent))
    pair_grad_own = after(scatter_far(pair_near), o_sent)
    pair_grad_b = jnp.concatenate(
        [rotate(pair_grad_own[:, :HEAD_SIZE], spots_own, -1.0), pair_grad_own[:, HEAD_SIZE:]],
        axis=1,
    ).astype(bf16)
    query_grad = (
        jnp.einsum("hqk,kd->qhd", score_grad_b, all_keys, preferred_element_type=f32) * score_scale
    )
    query_grad_b = rotate(query_grad, positions, -1.0).reshape(row_count, query_cols).astype(bf16)
    normed_grad = scatter_mp(dot_cols(query_grad_b, q_full)) + dot_cols(pair_grad_b, kv_full)
    unused_first, attn_pull = jax.vjp(rms_norm, tokens_own, attention_norm_gain)
    inputs_norm_grad, attn_gain_part = attn_pull(normed_grad)
    tokens_grad = gather_mp(middle_grad + inputs_norm_grad).reshape(row_count, model_width)

    query_grad_all = lax.all_gather(query_grad_b, "dp", axis=0, tiled=True)
    pair_grad_all = lax.all_gather(pair_grad_b, ("dp", "mp"), axis=0, tiled=True)
    q_weight_grad = dot_rows(normed_cols, query_grad_all)
    kv_weight_grad = dot_rows(normed_cols, after(pair_grad_all, mlp_branch))
    o_weight_grad = jnp.sum(o_sent.astype(f32), axis=0)
    q_weight_b = q_weight_grad.astype(bf16)
    kv_weight_b = kv_weight_grad.astype(bf16)
    o_weight_b = o_weight_grad.astype(bf16)
    qo_lora_a = sum_mp(
        jnp.concatenate([dot_cols(q_weight_b, q_right), dot_cols(o_weight_b, o_right)], axis=1)
    )
    kv_lora_a = jnp.concatenate(
        [
            dot_cols(kv_weight_b[:, :HEAD_SIZE], kv_right[:, :HEAD_SIZE]),
            dot_cols(kv_weight_b[:, HEAD_SIZE:], kv_right[:, HEAD_SIZE:]),
        ],
        axis=1,
    )
    right_parts = jnp.concatenate(
        [
            dot_rows(q_left, q_weight_b),
            dot_rows(o_left, o_weight_b),
            dot_rows(kv_left[:, :rank], kv_weight_b[:, :HEAD_SIZE]),
            dot_rows(kv_left[:, rank:], kv_weight_b[:, HEAD_SIZE:]),
        ],
        axis=1,
    ).astype(bf16)
    right_grads = jnp.sum(
        exchange(right_parts.reshape(dp_count, rank_own, -1)).astype(f32), axis=0
    )

    block_all = block_width + rank_own

    def side_by_side(arrived, first):
        return jnp.concatenate(
            [arrived[place, first : first + rank_own].astype(f32) for place in range(dp_count)],
            axis=1,
        )

    down_arrived = down_gate_sent[:, :block_all]
    gate_arrived = down_gate_sent[:, block_all:]
    down_weight_grad, down_lora_a = receive_grad(
        current_loop, down_arrived, down_update_right, block_width
    )
    gate_weight_grad, gate_lora_a = receive_grad(
        current_loop, gate_arrived, gate_update_right, block_width
    )
    up_weight_grad, up_lora_a = receive_grad(
        current_loop, up_sent, up_update_right, block_width
    )
    down_lora_b = side_by_side(down_arrived, block_width)
    gate_lora_b = side_by_side(gate_arrived, block_width)
    up_lora_b = side_by_side(up_sent, block_width)
    mlp_lora_a = sum_mp(jnp.concatenate([gate_lora_a, up_lora_a, down_lora_a], axis=1))

    small = sum_all(
        jnp.concatenate([attn_gain_part, mlp_gain_part, depth_own, confidence_own.reshape(1)])
    )
    gain_width = model_width // dp_count
    attn_gain_grad = lax.dynamic_slice_in_dim(small, dp_place * gain_width, gain_width, 0)
    mlp_gain_grad = lax.dynamic_slice_in_dim(
        small, model_width + dp_place * gain_width, gain_width, 0
    )
    counts = small[2 * model_width : 2 * model_width + LOOP_COUNT].astype(jnp.int32)
    confidence = small[2 * model_width + LOOP_COUNT :] / (row_count * dp_count)

    def place_loop(grad_item):
        chosen = jnp.arange(LOOP_COUNT)[:, None, None] == loop_selection
        return jnp.where(chosen, grad_item[None], 0.0)

    return (
        counts,
        confidence,
        mixed,
        tokens_grad,
        attn_gain_grad,
        mlp_gain_grad,
        q_weight_grad,
        kv_weight_grad,
        o_weight_grad,
        gate_weight_grad,
        up_weight_grad,
        down_weight_grad,
        place_loop(qo_lora_a[:, :rank]),
        place_loop(right_grads[:, :query_cols]),
        place_loop(kv_lora_a),
        place_loop(right_grads[:, 2 * query_cols :]),
        place_loop(qo_lora_a[:, rank:]),
        place_loop(right_grads[:, query_cols : 2 * query_cols]),
        place_loop(mlp_lora_a[:, :rank]),
        place_loop(gate_lora_b),
        place_loop(mlp_lora_a[:, rank : 2 * rank]),
        place_loop(up_lora_b),
        place_loop(mlp_lora_a[:, 2 * rank :]),
        place_loop(down_lora_b),
    )


def solution(mesh):
    return jax.shard_map(
        body,
        mesh=mesh,
        in_specs=(
            P("dp", None),
            P("dp", None),
            P("dp"),
            P("dp"),
            P("dp"),
            P(),
            P(),
            P(),
            P(),
            P("dp", "mp"),
            P("dp", None),
            P("dp", "mp"),
            P("dp", "mp"),
            P("dp", "mp"),
            P("dp", "mp"),
            P(None, "dp", None),
            P(None, None, "mp"),
            P(None, "dp", None),
            P(),
            P(None, "dp", None),
            P(None, None, "mp"),
            P(None, "dp", None),
            P(None, None, "mp"),
            P(None, "dp", None),
            P(None, None, "mp"),
            P(None, "dp", None),
            P(None, None, "mp"),
        ),
        out_specs=(
            P(),
            P(),
            P("dp", None),
            P("dp", None),
            P("dp"),
            P("dp"),
            P("dp", "mp"),
            P("dp", None),
            P("dp", "mp"),
            P("dp", "mp"),
            P("dp", "mp"),
            P("dp", "mp"),
            P(None, "dp", None),
            P(None, "dp", "mp"),
            P(None, "dp", None),
            P(None, "dp", None),
            P(None, "dp", None),
            P(None, "dp", "mp"),
            P(None, "dp", None),
            P(None, "dp", "mp"),
            P(None, "dp", None),
            P(None, "dp", "mp"),
            P(None, "dp", None),
            P(None, "dp", "mp"),
        ),
        check_vma=False,
    )
```

```python
import math

import jax
import jax.numpy as jnp
from jax import lax
from jax.experimental import pallas as pl
from jax.experimental.pallas import tpu as pltpu
from jax.sharding import PartitionSpec as P

HEAD_SIZE = 256
LOOP_COUNT = 3


EPSILON = 1e-06
MASKED_SCORE = -1e30
precise = lax.Precision.HIGHEST
f32 = jnp.float32
bf16 = jnp.bfloat16


def rms_norm(inputs, gain):
    return inputs * lax.rsqrt(jnp.mean(inputs * inputs, axis=-1, keepdims=True) + EPSILON) * gain


def rotate(inputs, spots, direction):
    half_width = inputs.shape[-1] // 2
    frequency = jnp.exp(
        jnp.arange(half_width, dtype=jnp.float32) * (-2.0 * math.log(10000.0) / inputs.shape[-1])
    )
    angles = spots.astype(jnp.float32)[:, None] * frequency[None, :]
    cos_part = jnp.cos(angles)
    sin_part = jnp.sin(angles) * direction
    if inputs.ndim == 3:
        cos_part = cos_part[:, None, :]
        sin_part = sin_part[:, None, :]
    first_half = inputs[..., :half_width]
    second_half = inputs[..., half_width:]
    return jnp.concatenate(
        [
            first_half * cos_part - second_half * sin_part,
            second_half * cos_part + first_half * sin_part,
        ],
        axis=-1,
    )


def update_delta(left_factor, right_factor, factor_pairs):
    if factor_pairs:
        rank_half = left_factor.shape[1] // 2
        width_half = right_factor.shape[1] // 2
        key_half = jnp.dot(
            left_factor[:, :rank_half],
            right_factor[:, :width_half],
            preferred_element_type=jnp.float32,
        )
        value_half = jnp.dot(
            left_factor[:, rank_half:],
            right_factor[:, width_half:],
            preferred_element_type=jnp.float32,
        )
        return jnp.concatenate([key_half, value_half], axis=1)
    return jnp.dot(left_factor, right_factor, preferred_element_type=jnp.float32)


def attention_weights(queries, key_rows, query_seq, query_spots, key_seq, key_spots, score_scale):
    scores = (
        jnp.einsum("qhd,kd->hqk", queries, key_rows, preferred_element_type=jnp.float32)
        * score_scale
    )
    allowed = (query_seq[:, None] == key_seq[None, :]) & (
        key_spots[None, :] <= query_spots[:, None]
    )
    scores = jnp.where(allowed[None], scores, MASKED_SCORE)
    return jax.nn.softmax(scores, axis=-1)


def dot(left, right):
    return jnp.dot(left, right, preferred_element_type=f32)


def dot_rows(left, right):
    return lax.dot_general(left, right, (((0,), (0,)), ((), ())), preferred_element_type=f32)


def dot_cols(left, right):
    return lax.dot_general(left, right, (((1,), (1,)), ((), ())), preferred_element_type=f32)


def swap(value, axis, bit):
    count = lax.axis_size(axis)
    return lax.ppermute(value, axis, [(place, place ^ bit) for place in range(count)])


def exchange(blocks):
    return lax.all_to_all(blocks, "dp", 0, 0, tiled=True)


def far_bits():
    bit = lax.axis_size("dp") // 2
    bits = []
    while bit > 1:
        bits.append(bit)
        bit = bit // 2
    return bits


def grow(value, axis, bit):
    return jnp.concatenate([value, swap(value, axis, bit)], axis=0)


def fold(value, axis, bit):
    half = value.shape[0] // 2
    arrived = swap(value[half:].astype(bf16), axis, bit)
    return value[:half] + arrived.astype(f32)


def after(value, *others):
    total = jnp.zeros((), f32)
    for other in others:
        last = other[tuple(size - 1 for size in other.shape)]
        total = jnp.maximum(total, jnp.abs(last.astype(f32)))
    return value + jnp.minimum(total, 0.0).astype(value.dtype)


def halves(value):
    half = value.shape[0] // 2
    return value[:half], value[half:]


def gather_mp(value):
    place = lax.axis_index("mp")
    arrived = swap(value, "mp", 2)
    value = jnp.where(
        place < 2, jnp.stack([value, arrived], axis=0), jnp.stack([arrived, value], axis=0)
    )
    arrived = swap(value, "mp", 1)
    return jnp.where(
        place % 2 == 0, jnp.stack([value, arrived], axis=1), jnp.stack([arrived, value], axis=1)
    )


def scatter_mp(value):
    place = lax.axis_index("mp")
    for axis, bit, own in ((1, 1, place % 2), (0, 2, place // 2)):
        if axis == 1:
            value = value.reshape((2, 2, value.shape[0] // 4) + value.shape[1:])
        sent = lax.dynamic_index_in_dim(value, 1 - own, axis, keepdims=False)
        kept = lax.dynamic_index_in_dim(value, own, axis, keepdims=False)
        value = kept + swap(sent.astype(bf16), "mp", bit).astype(f32)
    return value


def gather_far(value):
    for bit in far_bits():
        value = grow(value, "dp", bit)
    return value


def gather_near(value):
    half = value.shape[0] // 2
    front = grow(grow(value[:half], "dp", 1), "mp", 2)
    rear = grow(grow(value[half:], "mp", 2), "dp", 1)
    return jnp.concatenate([front, rear], axis=0)


def other_core(value):
    return swap(value, "mp", 1)


def add_core(sent, kept):
    return kept + swap(sent.astype(bf16), "mp", 1).astype(f32)


def scatter_near(value):
    value = value.astype(f32)
    half = value.shape[0] // 2
    front = fold(fold(value[:half], "mp", 2), "dp", 1)
    rear = fold(fold(value[half:], "dp", 1), "mp", 2)
    return jnp.concatenate([front, rear], axis=0)


def scatter_far(value):
    for bit in reversed(far_bits()):
        value = fold(value, "dp", bit)
    return value


def sum_all(value):
    for axis in ("mp", "dp"):
        bit = 1
        while bit < lax.axis_size(axis):
            value = value + swap(value, axis, bit)
            bit = bit * 2
    return value


def sum_mp(value):
    value = value + swap(value, "mp", 1)
    low = value.astype(bf16)
    return low.astype(f32) + swap(low, "mp", 2).astype(f32)


def merge_kernel(loop_ref, *refs):
    out_ref = refs[-1]
    width = refs[0].shape[1]
    for index in range(len(refs) // 3):
        base_ref, left_ref, right_ref = refs[3 * index : 3 * index + 3]
        delta = jnp.dot(left_ref[0], right_ref[0], preferred_element_type=f32)
        merged = base_ref[...].astype(f32) + delta
        out_ref[0, :, index * width : (index + 1) * width] = merged.astype(bf16)


def merge_blocks(loop, places, weights):
    rows, columns = weights[0][0].shape
    rank = weights[0][1].shape[2]
    width = columns // places
    specs = []
    arrays = []
    for base, left, right in weights:
        specs.append(pl.BlockSpec((rows, width), lambda place, loop_ref: (0, place)))
        specs.append(pl.BlockSpec((1, rows, rank), lambda place, loop_ref: (loop_ref[0], 0, 0)))
        specs.append(
            pl.BlockSpec((1, rank, width), lambda place, loop_ref: (loop_ref[0], 0, place))
        )
        arrays += [base, left, right]
    return pl.pallas_call(
        merge_kernel,
        out_shape=jax.ShapeDtypeStruct((places, rows, width * len(weights)), bf16),
        grid_spec=pltpu.PrefetchScalarGridSpec(
            num_scalar_prefetch=1,
            grid=(places,),
            in_specs=specs,
            out_specs=pl.BlockSpec(
                (1, rows, width * len(weights)), lambda place, loop_ref: (place, 0, 0)
            ),
        ),
        compiler_params=pltpu.CompilerParams(vmem_limit_bytes=48 * 2**20),
    )(loop, *arrays)


def receive_kernel(loop_ref, arrived_ref, right_ref, grad_ref, left_grad_ref, right_grad_ref):
    rows = grad_ref.shape[0]
    width = arrived_ref.shape[2]
    total = None
    for place in range(arrived_ref.shape[0]):
        columns = slice(place * width, (place + 1) * width)
        block = arrived_ref[place, :rows, :]
        grad_ref[:, columns] = block.astype(f32)
        part = lax.dot_general(
            block, right_ref[0, :, columns], (((1,), (1,)), ((), ())), preferred_element_type=f32
        )
        total = part if total is None else total + part
        right_grad = arrived_ref[place, rows:, :].astype(f32)
        for loop in range(LOOP_COUNT):
            right_grad_ref[loop, :, columns] = jnp.where(loop_ref[0] == loop, right_grad, 0.0)

    @pl.when(pl.program_id(0) == 0)
    def first():
        left_grad_ref[...] = total

    @pl.when(pl.program_id(0) > 0)
    def later():
        left_grad_ref[...] += total


def receive_grad(loop, arrived, which, all_rows, right, rows):
    places, _, width = arrived.shape
    rank = right.shape[1]
    step = 2
    return pl.pallas_call(
        receive_kernel,
        out_shape=(
            jax.ShapeDtypeStruct((rows, places * width), f32),
            jax.ShapeDtypeStruct((rows, rank), f32),
            jax.ShapeDtypeStruct((LOOP_COUNT, all_rows - rows, places * width), f32),
        ),
        grid_spec=pltpu.PrefetchScalarGridSpec(
            num_scalar_prefetch=1,
            grid=(places // step,),
            in_specs=[
                pl.BlockSpec((step, all_rows, width), lambda place, loop_ref: (place, which, 0)),
                pl.BlockSpec(
                    (1, rank, step * width), lambda place, loop_ref: (loop_ref[0], 0, place)
                ),
            ],
            out_specs=(
                pl.BlockSpec((rows, step * width), lambda place, loop_ref: (0, place)),
                pl.BlockSpec((rows, rank), lambda place, loop_ref: (0, 0)),
                pl.BlockSpec(
                    (LOOP_COUNT, all_rows - rows, step * width),
                    lambda place, loop_ref: (0, 0, place),
                ),
            ),
        ),
        compiler_params=pltpu.CompilerParams(vmem_limit_bytes=48 * 2**20),
    )(loop, arrived, right)


def feed_kernel(normed_ref, cotangent_ref, *refs):
    weights, outs = refs[:-4], refs[-4:]
    hidden_ref, grads_ref, partial_ref, branch_ref = outs
    normed = normed_ref[...]
    cotangent = cotangent_ref[...]
    scale = math.sqrt(2.0 / math.pi)
    partial = None
    for index in range(len(weights) // 2):
        gate_down_ref, up_ref = weights[2 * index : 2 * index + 2]
        width = up_ref.shape[1]
        gate_act = jnp.dot(normed, gate_down_ref[:, :width], preferred_element_type=f32)
        up_act = jnp.dot(normed, up_ref[...], preferred_element_type=f32)
        hidden_grad = jnp.dot(cotangent, gate_down_ref[:, width:], preferred_element_type=f32)
        square = gate_act * gate_act
        tanh_part = jnp.tanh(scale * (gate_act + 0.044715 * (gate_act * square)))
        half_sum = 0.5 * (1.0 + tanh_part)
        gelu = gate_act * half_sum
        slope = half_sum + (0.5 * gate_act) * (1.0 - tanh_part * tanh_part) * (
            scale * (1.0 + (3.0 * 0.044715) * square)
        )
        hidden = (gelu * up_act).astype(bf16)
        gate_grad = (hidden_grad * up_act * slope).astype(bf16)
        up_grad = (hidden_grad * gelu).astype(bf16)
        hidden_ref[:, index * width : (index + 1) * width] = hidden
        grads_ref[:, 2 * index * width : (2 * index + 1) * width] = gate_grad
        grads_ref[:, (2 * index + 1) * width : (2 * index + 2) * width] = up_grad
        sums = [
            lax.dot_general(
                left, right, (((1,), (1,)), ((), ())), preferred_element_type=f32
            )
            for left, right in (
                (gate_grad, gate_down_ref[:, :width]),
                (up_grad, up_ref[...]),
                (hidden, gate_down_ref[:, width:]),
            )
        ]
        if partial is None:
            partial = sums[0] + sums[1]
            branch = sums[2]
        else:
            partial = partial + sums[0] + sums[1]
            branch = branch + sums[2]
    partial_ref[...] = partial
    branch_ref[...] = branch.astype(bf16)


def feed_forward(normed, cotangent, weights):
    rows, model_width = normed.shape
    width = weights[1].shape[1]
    pairs = len(weights) // 2
    tile = math.gcd(rows, 256)
    row_block = pl.BlockSpec((tile, model_width), lambda step: (step, 0))
    return pl.pallas_call(
        feed_kernel,
        out_shape=(
            jax.ShapeDtypeStruct((rows, pairs * width), bf16),
            jax.ShapeDtypeStruct((rows, 2 * pairs * width), bf16),
            jax.ShapeDtypeStruct((rows, model_width), f32),
            jax.ShapeDtypeStruct((rows, model_width), bf16),
        ),
        grid=(rows // tile,),
        in_specs=[row_block, row_block]
        + [
            pl.BlockSpec(
                weight.shape, lambda step: (0, 0), pipeline_mode=pl.Buffered(1)
            )
            for weight in weights
        ],
        out_specs=(
            pl.BlockSpec((tile, pairs * width), lambda step: (step, 0)),
            pl.BlockSpec((tile, 2 * pairs * width), lambda step: (step, 0)),
            row_block,
            row_block,
        ),
        compiler_params=pltpu.CompilerParams(vmem_limit_bytes=56 * 2**20),
    )(normed, cotangent, *weights)


def body(
    tokens,
    cotangent,
    token_sequence_index,
    positions,
    token_exit_loop,
    current_loop,
    attention_norm_gain,
    feedforward_norm_gain,
    probe,
    query_matrix,
    key_value_matrix,
    output_matrix,
    gate_matrix,
    up_matrix,
    down_matrix,
    query_update_left,
    query_update_right,
    key_value_update_left,
    key_value_update_right,
    output_update_left,
    output_update_right,
    gate_update_left,
    gate_update_right,
    up_update_left,
    up_update_right,
    down_update_left,
    down_update_right,
):
    loop_selection = current_loop[0]
    score_scale = HEAD_SIZE ** (-0.5)
    mp_count = lax.axis_size("mp")
    dp_count = lax.axis_size("dp")
    mp_place = lax.axis_index("mp")
    dp_place = lax.axis_index("dp")
    row_count, model_width = tokens.shape
    own_rows = row_count // mp_count
    block_width, query_cols = query_matrix.shape
    head_count = query_cols // HEAD_SIZE
    hidden_own = gate_matrix.shape[1] // dp_count
    rank = gate_update_left.shape[2]
    rank_own = rank // dp_count

    def pick(table):
        return lax.dynamic_index_in_dim(table, loop_selection, 0, keepdims=False)

    q_left, kv_left, o_left = map(
        pick, (query_update_left, key_value_update_left, output_update_left)
    )
    gate_left, up_left, down_left = map(pick, (gate_update_left, up_update_left, down_update_left))
    q_right, kv_right, o_right = map(
        pick, (query_update_right, key_value_update_right, output_update_right)
    )
    def merge(base, left, right, pairs=False):
        return (base.astype(f32) + update_delta(left, right, pairs)).astype(bf16)

    def own_slice(value):
        return lax.dynamic_slice_in_dim(value, mp_place * own_rows, own_rows, 0)

    def to_places(shard, width):
        blocks = [shard[:, place * width : (place + 1) * width] for place in range(dp_count)]
        return jnp.stack(blocks, axis=0)

    block_rows = block_width // mp_count

    def block_slice(value):
        return lax.dynamic_slice_in_dim(value, mp_place * block_rows, block_rows, 0)

    kv_full = lax.all_gather(
        merge(block_slice(key_value_matrix), block_slice(kv_left), kv_right, True),
        ("dp", "mp"),
        axis=0,
        tiled=True,
    )
    q_o_full = lax.all_gather(
        jnp.concatenate(
            [merge(query_matrix, q_left, q_right), merge(output_matrix, o_left, o_right)], axis=1
        ),
        "dp",
        axis=0,
        tiled=True,
    )
    q_full = q_o_full[:, :query_cols]
    o_full = q_o_full[:, query_cols:]

    cotangent_own = own_slice(cotangent)
    cotangent_rows = gather_near(gather_far(cotangent_own))

    tokens_own = own_slice(tokens).astype(f32)
    normed_b = rms_norm(tokens.astype(f32), attention_norm_gain).astype(bf16)

    def all_token_cols(rows_own, *others):
        cols = exchange(after(to_places(rows_own, block_width), *others))
        cols = cols.reshape(-1, block_width)
        cols = gather_mp(cols).reshape(mp_count, dp_count, own_rows, block_width)
        return jnp.swapaxes(cols, 0, 1).reshape(dp_count * row_count, block_width)

    normed_cols = all_token_cols(own_slice(normed_b))
    pair_own = dot(own_slice(normed_b), kv_full)
    seq_own = own_slice(token_sequence_index)
    spots_own = own_slice(positions)
    marks = jnp.stack([seq_own, spots_own // 64, spots_own % 64], axis=0).astype(bf16)
    marks = jnp.pad(marks, ((0, 5), (0, 2 * HEAD_SIZE - own_rows)))
    outgoing = jnp.concatenate(
        [
            rotate(pair_own[:, :HEAD_SIZE], spots_own, 1.0).astype(bf16),
            pair_own[:, HEAD_SIZE:].astype(bf16),
        ],
        axis=1,
    )
    outgoing = jnp.concatenate([outgoing, marks], axis=0)
    pairs_far = after(gather_far(outgoing), *halves(cotangent_rows))
    pairs_front = gather_near(pairs_far)
    all_pairs = jnp.concatenate([pairs_front, other_core(pairs_front)], axis=0)
    all_pairs = all_pairs.reshape(-1, own_rows + 8, 2 * HEAD_SIZE)
    all_keys = all_pairs[:, :own_rows, :HEAD_SIZE].reshape(-1, HEAD_SIZE)
    all_values = all_pairs[:, :own_rows, HEAD_SIZE:].reshape(-1, HEAD_SIZE)
    all_marks = all_pairs[:, own_rows : own_rows + 3, :own_rows].astype(jnp.int32)
    all_seq = all_marks[:, 0].reshape(-1)
    all_spots = (all_marks[:, 1] * 64 + all_marks[:, 2]).reshape(-1)
    queries = dot(normed_b, q_full)
    query_b = rotate(queries.reshape(row_count, head_count, HEAD_SIZE), positions, 1.0).astype(
        bf16
    )
    gate_down = exchange(
        merge_blocks(
            after(current_loop, *halves(pairs_front)),
            dp_count,
            [
                (gate_matrix, gate_update_left, gate_update_right),
                (down_matrix, down_update_left, down_update_right),
            ],
        )
    ).reshape(model_width, 2 * hidden_own)
    query_b = after(query_b, normed_cols)
    weights_soft = attention_weights(
        query_b, all_keys, token_sequence_index, positions, all_seq, all_spots, score_scale
    )
    weights_low = weights_soft.astype(bf16)
    attended = jnp.einsum("hqk,kd->qhd", weights_low, all_values, preferred_element_type=f32)
    attended_b = attended.reshape(row_count, query_cols).astype(bf16)
    middle = tokens_own + scatter_mp(dot_cols(attended_b, o_full))
    normed2_b = rms_norm(middle, feedforward_norm_gain).astype(bf16)

    normed2_far = gather_far(after(normed2_b, gate_down))
    up_own = exchange(
        merge_blocks(
            after(current_loop, normed2_far),
            dp_count,
            [(up_matrix, up_update_left, up_update_right)],
        )
    ).reshape(model_width, hidden_own)
    normed2_rows = gather_near(normed2_far)
    attended_all = lax.all_gather(attended_b, "dp", axis=0, tiled=True)
    left_block = jnp.concatenate([gate_left, up_left, down_left], axis=1)
    left_all = lax.all_gather(
        after(block_slice(left_block), gate_down), ("dp", "mp"), axis=0, tiled=True
    )
    gate_down_other = swap(gate_down, "mp", 1)
    up_other = swap(after(up_own, *halves(normed2_rows)), "mp", 1)
    hidden_b, unit_grad_b, partial, branch_part = feed_forward(
        normed2_rows, cotangent_rows, (gate_down, up_own, gate_down_other, up_other)
    )
    normed2_near = scatter_near(partial)

    def weight_grad(rows, grads, width):
        sent = dot_rows(rows, grads[:, width:]).astype(bf16)
        kept = dot_rows(rows, grads[:, :width])
        return (kept + swap(sent, "mp", 1).astype(f32)).astype(bf16)

    def to_blocks(grad_b, left_cols):
        right_part = dot_rows(left_cols, grad_b).astype(bf16)
        return [
            grad_b.reshape(dp_count, block_width, hidden_own),
            right_part.reshape(dp_count, rank_own, hidden_own),
        ]

    down_grad_b = weight_grad(cotangent_rows, hidden_b, hidden_own)
    gate_up_grad_b = weight_grad(normed2_rows, unit_grad_b, 2 * hidden_own)
    down_sent = exchange(
        jnp.concatenate(to_blocks(down_grad_b, after(left_all[:, 2 * rank :], attended_all)), axis=1)
    )
    gate_up_blocks = jnp.concatenate(
        to_blocks(gate_up_grad_b[:, :hidden_own], left_all[:, :rank])
        + to_blocks(gate_up_grad_b[:, hidden_own:], left_all[:, rank : 2 * rank]),
        axis=1,
    )
    normed2_grad = scatter_far(after(normed2_near, down_sent, gate_up_blocks))
    gate_up_sent = exchange(after(gate_up_blocks, normed2_grad))

    unused_norm, mlp_pull = jax.vjp(rms_norm, middle, feedforward_norm_gain)
    middle_norm_grad, mlp_gain_part = mlp_pull(normed2_grad)
    middle_grad = cotangent_own.astype(f32) + middle_norm_grad
    branch_grad_own = middle_grad.astype(bf16)
    branch_grad = gather_mp(branch_grad_own).reshape(row_count, model_width)
    attended_grad_b = (
        dot(branch_grad, o_full).astype(bf16).reshape(row_count, head_count, HEAD_SIZE)
    )
    prob_grad = jnp.einsum("qhd,kd->hqk", attended_grad_b, all_values, preferred_element_type=f32)
    score_grad_b = (
        weights_soft * (prob_grad - jnp.sum(prob_grad * weights_soft, axis=-1, keepdims=True))
    ).astype(bf16)
    keys_grad = (
        jnp.einsum("hqk,qhd->kd", score_grad_b, query_b, preferred_element_type=f32) * score_scale
    )
    values_grad = jnp.einsum(
        "hqk,qhd->kd", weights_low, attended_grad_b, preferred_element_type=f32
    )
    pair_partial = jnp.concatenate([keys_grad, values_grad], axis=1)
    half = pair_partial.shape[0] // 2
    block_all = block_width + rank_own

    down_weight_grad, down_lora_a, down_lora_b = receive_grad(
        after(current_loop, attended_grad_b), down_sent, 0, block_all, down_update_right, block_width
    )
    pair_near = scatter_near(add_core(pair_partial[half:], pair_partial[:half]))
    branch_near = scatter_near(after(branch_part, normed2_grad))
    query_grad = (
        jnp.einsum("hqk,kd->qhd", score_grad_b, all_keys, preferred_element_type=f32) * score_scale
    )
    query_grad_b = rotate(query_grad, positions, -1.0).reshape(row_count, query_cols).astype(bf16)
    query_grad_all = lax.all_gather(query_grad_b, "dp", axis=0, tiled=True)
    branch_cols = all_token_cols(branch_grad_own, gate_up_sent)
    q_weight_grad = dot_rows(normed_cols, query_grad_all)
    o_weight_grad = dot_rows(branch_cols, attended_all)
    q_weight_b = q_weight_grad.astype(bf16)
    o_weight_b = o_weight_grad.astype(bf16)
    qo_lora_a = sum_mp(
        jnp.concatenate([dot_cols(q_weight_b, q_right), dot_cols(o_weight_b, o_right)], axis=1)
    )
    qo_right = jnp.concatenate(
        [dot_rows(q_left, q_weight_b), dot_rows(o_left, o_weight_b)], axis=1
    ).astype(bf16)
    pair_grad_own = scatter_far(
        after(pair_near, gate_up_sent, qo_right, qo_lora_a, *halves(branch_near))
    )
    pair_grad_b = jnp.concatenate(
        [rotate(pair_grad_own[:, :HEAD_SIZE], spots_own, -1.0), pair_grad_own[:, HEAD_SIZE:]],
        axis=1,
    ).astype(bf16)
    mlp_branch = scatter_far(after(branch_near, *halves(pair_near)))
    output_rows = middle + mlp_branch
    mixed = gather_mp(output_rows.astype(bf16)).reshape(row_count, model_width)
    confidence_own = jnp.sum(jax.nn.sigmoid(jnp.dot(output_rows, probe, precision=precise)))
    levels = jnp.arange(LOOP_COUNT, dtype=jnp.int32)
    exit_own = own_slice(token_exit_loop)
    depth_own = jnp.sum((exit_own[:, None] == levels[None, :]).astype(f32), axis=0)

    normed_grad = scatter_mp(dot_cols(query_grad_b, q_full)) + dot_cols(pair_grad_b, kv_full)
    unused_first, attn_pull = jax.vjp(rms_norm, tokens_own, attention_norm_gain)
    inputs_norm_grad, attn_gain_part = attn_pull(normed_grad)
    tokens_grad = gather_mp(middle_grad + inputs_norm_grad).reshape(row_count, model_width)

    pair_grad_all = lax.all_gather(pair_grad_b, ("dp", "mp"), axis=0, tiled=True)
    small = sum_all(
        jnp.concatenate([attn_gain_part, mlp_gain_part, depth_own, confidence_own.reshape(1)])
    )
    kv_weight_grad = dot_rows(normed_cols, after(pair_grad_all, small, tokens_grad))
    kv_weight_b = kv_weight_grad.astype(bf16)
    kv_lora_a = jnp.concatenate(
        [
            dot_cols(kv_weight_b[:, :HEAD_SIZE], kv_right[:, :HEAD_SIZE]),
            dot_cols(kv_weight_b[:, HEAD_SIZE:], kv_right[:, HEAD_SIZE:]),
        ],
        axis=1,
    )
    right_parts = jnp.concatenate(
        [
            qo_right,
            dot_rows(kv_left[:, :rank], kv_weight_b[:, :HEAD_SIZE]).astype(bf16),
            dot_rows(kv_left[:, rank:], kv_weight_b[:, HEAD_SIZE:]).astype(bf16),
        ],
        axis=1,
    )
    right_grads = jnp.sum(
        exchange(right_parts.reshape(dp_count, rank_own, -1)).astype(f32), axis=0
    )

    late_loop = after(current_loop, pair_grad_own)
    gate_weight_grad, gate_lora_a, gate_lora_b = receive_grad(
        late_loop, gate_up_sent, 0, block_all, gate_update_right, block_width
    )
    up_weight_grad, up_lora_a, up_lora_b = receive_grad(
        late_loop, gate_up_sent, 1, block_all, up_update_right, block_width
    )
    mlp_lora_a = sum_mp(jnp.concatenate([gate_lora_a, up_lora_a, down_lora_a], axis=1))

    gain_width = model_width // dp_count
    attn_gain_grad = lax.dynamic_slice_in_dim(small, dp_place * gain_width, gain_width, 0)
    mlp_gain_grad = lax.dynamic_slice_in_dim(
        small, model_width + dp_place * gain_width, gain_width, 0
    )
    counts = small[2 * model_width : 2 * model_width + LOOP_COUNT].astype(jnp.int32)
    confidence = small[2 * model_width + LOOP_COUNT :] / (row_count * dp_count)

    def place_loop(grad_item):
        chosen = jnp.arange(LOOP_COUNT)[:, None, None] == loop_selection
        return jnp.where(chosen, grad_item[None], 0.0)

    return (
        counts,
        confidence,
        mixed,
        tokens_grad,
        attn_gain_grad,
        mlp_gain_grad,
        q_weight_grad,
        kv_weight_grad,
        o_weight_grad,
        gate_weight_grad,
        up_weight_grad,
        down_weight_grad,
        place_loop(qo_lora_a[:, :rank]),
        place_loop(right_grads[:, :query_cols]),
        place_loop(kv_lora_a),
        place_loop(right_grads[:, 2 * query_cols :]),
        place_loop(qo_lora_a[:, rank:]),
        place_loop(right_grads[:, query_cols : 2 * query_cols]),
        place_loop(mlp_lora_a[:, :rank]),
        gate_lora_b,
        place_loop(mlp_lora_a[:, rank : 2 * rank]),
        up_lora_b,
        place_loop(mlp_lora_a[:, 2 * rank :]),
        down_lora_b,
    )


def solution(mesh):
    return jax.shard_map(
        body,
        mesh=mesh,
        in_specs=(
            P("dp", None),
            P("dp", None),
            P("dp"),
            P("dp"),
            P("dp"),
            P(),
            P(),
            P(),
            P(),
            P("dp", "mp"),
            P("dp", None),
            P("dp", "mp"),
            P("dp", "mp"),
            P("dp", "mp"),
            P("dp", "mp"),
            P(None, "dp", None),
            P(None, None, "mp"),
            P(None, "dp", None),
            P(),
            P(None, "dp", None),
            P(None, None, "mp"),
            P(None, "dp", None),
            P(None, None, "mp"),
            P(None, "dp", None),
            P(None, None, "mp"),
            P(None, "dp", None),
            P(None, None, "mp"),
        ),
        out_specs=(
            P(),
            P(),
            P("dp", None),
            P("dp", None),
            P("dp"),
            P("dp"),
            P("dp", "mp"),
            P("dp", None),
            P("dp", "mp"),
            P("dp", "mp"),
            P("dp", "mp"),
            P("dp", "mp"),
            P(None, "dp", None),
            P(None, "dp", "mp"),
            P(None, "dp", None),
            P(None, "dp", None),
            P(None, "dp", None),
            P(None, "dp", "mp"),
            P(None, "dp", None),
            P(None, "dp", "mp"),
            P(None, "dp", None),
            P(None, "dp", "mp"),
            P(None, "dp", None),
            P(None, "dp", "mp"),
        ),
        check_vma=False,
    )
```

```python
import math

import jax
import jax.numpy as jnp
from jax import lax
from jax.experimental import pallas as pl
from jax.experimental.pallas import tpu as pltpu
from jax.sharding import PartitionSpec as P

HEAD_SIZE = 256
LOOP_COUNT = 3


EPSILON = 1e-06
MASKED_SCORE = -1e30
precise = lax.Precision.HIGHEST
f32 = jnp.float32
bf16 = jnp.bfloat16


def rms_norm(inputs, gain):
    return inputs * lax.rsqrt(jnp.mean(inputs * inputs, axis=-1, keepdims=True) + EPSILON) * gain


def rotate(inputs, spots, direction):
    half_width = inputs.shape[-1] // 2
    frequency = jnp.exp(
        jnp.arange(half_width, dtype=jnp.float32) * (-2.0 * math.log(10000.0) / inputs.shape[-1])
    )
    angles = spots.astype(jnp.float32)[:, None] * frequency[None, :]
    cos_part = jnp.cos(angles)
    sin_part = jnp.sin(angles) * direction
    if inputs.ndim == 3:
        cos_part = cos_part[:, None, :]
        sin_part = sin_part[:, None, :]
    first_half = inputs[..., :half_width]
    second_half = inputs[..., half_width:]
    return jnp.concatenate(
        [
            first_half * cos_part - second_half * sin_part,
            second_half * cos_part + first_half * sin_part,
        ],
        axis=-1,
    )


def update_delta(left_factor, right_factor, factor_pairs):
    if factor_pairs:
        rank_half = left_factor.shape[1] // 2
        width_half = right_factor.shape[1] // 2
        key_half = jnp.dot(
            left_factor[:, :rank_half],
            right_factor[:, :width_half],
            preferred_element_type=jnp.float32,
        )
        value_half = jnp.dot(
            left_factor[:, rank_half:],
            right_factor[:, width_half:],
            preferred_element_type=jnp.float32,
        )
        return jnp.concatenate([key_half, value_half], axis=1)
    return jnp.dot(left_factor, right_factor, preferred_element_type=jnp.float32)


def attention_weights(queries, key_rows, query_seq, query_spots, key_seq, key_spots, score_scale):
    scores = (
        jnp.einsum("qhd,kd->hqk", queries, key_rows, preferred_element_type=jnp.float32)
        * score_scale
    )
    allowed = (query_seq[:, None] == key_seq[None, :]) & (
        key_spots[None, :] <= query_spots[:, None]
    )
    scores = jnp.where(allowed[None], scores, MASKED_SCORE)
    return jax.nn.softmax(scores, axis=-1)


def dot(left, right):
    return jnp.dot(left, right, preferred_element_type=f32)


def dot_rows(left, right):
    return lax.dot_general(left, right, (((0,), (0,)), ((), ())), preferred_element_type=f32)


def dot_cols(left, right):
    return lax.dot_general(left, right, (((1,), (1,)), ((), ())), preferred_element_type=f32)


def swap(value, axis, bit):
    count = lax.axis_size(axis)
    return lax.ppermute(value, axis, [(place, place ^ bit) for place in range(count)])


def exchange(blocks):
    return lax.all_to_all(blocks, "dp", 0, 0, tiled=True)


def far_bits():
    bit = lax.axis_size("dp") // 2
    bits = []
    while bit > 1:
        bits.append(bit)
        bit = bit // 2
    return bits


def grow(value, axis, bit):
    return jnp.concatenate([value, swap(value, axis, bit)], axis=0)


def fold(value, axis, bit):
    half = value.shape[0] // 2
    arrived = swap(value[half:].astype(bf16), axis, bit)
    return value[:half] + arrived.astype(f32)


def after(value, *others):
    total = jnp.zeros((), f32)
    for other in others:
        last = other[tuple(size - 1 for size in other.shape)]
        total = jnp.maximum(total, jnp.abs(last.astype(f32)))
    return value + jnp.minimum(total, 0.0).astype(value.dtype)


def halves(value):
    half = value.shape[0] // 2
    return value[:half], value[half:]


def gather_mp(value):
    place = lax.axis_index("mp")
    arrived = swap(value, "mp", 2)
    value = jnp.where(
        place < 2, jnp.stack([value, arrived], axis=0), jnp.stack([arrived, value], axis=0)
    )
    arrived = swap(value, "mp", 1)
    return jnp.where(
        place % 2 == 0, jnp.stack([value, arrived], axis=1), jnp.stack([arrived, value], axis=1)
    )


def scatter_mp(value):
    place = lax.axis_index("mp")
    for axis, bit, own in ((1, 1, place % 2), (0, 2, place // 2)):
        if axis == 1:
            value = value.reshape((2, 2, value.shape[0] // 4) + value.shape[1:])
        sent = lax.dynamic_index_in_dim(value, 1 - own, axis, keepdims=False)
        kept = lax.dynamic_index_in_dim(value, own, axis, keepdims=False)
        value = kept + swap(sent.astype(bf16), "mp", bit).astype(f32)
    return value


def gather_far(value):
    for bit in far_bits():
        value = grow(value, "dp", bit)
    return value


def gather_near(value):
    half = value.shape[0] // 2
    front = grow(grow(value[:half], "dp", 1), "mp", 2)
    rear = grow(grow(value[half:], "mp", 2), "dp", 1)
    return jnp.concatenate([front, rear], axis=0)


def other_core(value):
    return swap(value, "mp", 1)


def add_core(sent, kept):
    return kept + swap(sent.astype(bf16), "mp", 1).astype(f32)


def scatter_near(value):
    value = value.astype(f32)
    half = value.shape[0] // 2
    front = fold(fold(value[:half], "mp", 2), "dp", 1)
    rear = fold(fold(value[half:], "dp", 1), "mp", 2)
    return jnp.concatenate([front, rear], axis=0)


def scatter_far(value):
    for bit in reversed(far_bits()):
        value = fold(value, "dp", bit)
    return value


def sum_all(value):
    for axis in ("mp", "dp"):
        bit = 1
        while bit < lax.axis_size(axis):
            value = value + swap(value, axis, bit)
            bit = bit * 2
    return value


def sum_mp(value):
    value = value + swap(value, "mp", 1)
    low = value.astype(bf16)
    return low.astype(f32) + swap(low, "mp", 2).astype(f32)


def merge_kernel(loop_ref, *refs):
    out_ref = refs[-1]
    width = refs[0].shape[1]
    for index in range(len(refs) // 3):
        base_ref, left_ref, right_ref = refs[3 * index : 3 * index + 3]
        delta = jnp.dot(left_ref[0], right_ref[0], preferred_element_type=f32)
        merged = base_ref[...].astype(f32) + delta
        out_ref[0, :, index * width : (index + 1) * width] = merged.astype(bf16)


def merge_blocks(loop, places, weights):
    rows, columns = weights[0][0].shape
    rank = weights[0][1].shape[2]
    width = columns // places
    specs = []
    arrays = []
    for base, left, right in weights:
        specs.append(pl.BlockSpec((rows, width), lambda place, loop_ref: (0, place)))
        specs.append(pl.BlockSpec((1, rows, rank), lambda place, loop_ref: (loop_ref[0], 0, 0)))
        specs.append(
            pl.BlockSpec((1, rank, width), lambda place, loop_ref: (loop_ref[0], 0, place))
        )
        arrays += [base, left, right]
    return pl.pallas_call(
        merge_kernel,
        out_shape=jax.ShapeDtypeStruct((places, rows, width * len(weights)), bf16),
        grid_spec=pltpu.PrefetchScalarGridSpec(
            num_scalar_prefetch=1,
            grid=(places,),
            in_specs=specs,
            out_specs=pl.BlockSpec(
                (1, rows, width * len(weights)), lambda place, loop_ref: (place, 0, 0)
            ),
        ),
        compiler_params=pltpu.CompilerParams(vmem_limit_bytes=48 * 2**20),
    )(loop, *arrays)


def receive_kernel(loop_ref, arrived_ref, right_ref, grad_ref, left_grad_ref, right_grad_ref):
    rows = grad_ref.shape[0]
    width = arrived_ref.shape[2]
    total = None
    for place in range(arrived_ref.shape[0]):
        columns = slice(place * width, (place + 1) * width)
        block = arrived_ref[place, :rows, :]
        grad_ref[:, columns] = block.astype(f32)
        part = lax.dot_general(
            block, right_ref[0, :, columns], (((1,), (1,)), ((), ())), preferred_element_type=f32
        )
        total = part if total is None else total + part
        right_grad = arrived_ref[place, rows:, :].astype(f32)
        for loop in range(LOOP_COUNT):
            right_grad_ref[loop, :, columns] = jnp.where(loop_ref[0] == loop, right_grad, 0.0)

    @pl.when(pl.program_id(0) == 0)
    def first():
        left_grad_ref[...] = total

    @pl.when(pl.program_id(0) > 0)
    def later():
        left_grad_ref[...] += total


def receive_grad(loop, arrived, which, all_rows, right, rows):
    places, _, width = arrived.shape
    rank = right.shape[1]
    step = 2
    return pl.pallas_call(
        receive_kernel,
        out_shape=(
            jax.ShapeDtypeStruct((rows, places * width), f32),
            jax.ShapeDtypeStruct((rows, rank), f32),
            jax.ShapeDtypeStruct((LOOP_COUNT, all_rows - rows, places * width), f32),
        ),
        grid_spec=pltpu.PrefetchScalarGridSpec(
            num_scalar_prefetch=1,
            grid=(places // step,),
            in_specs=[
                pl.BlockSpec((step, all_rows, width), lambda place, loop_ref: (place, which, 0)),
                pl.BlockSpec(
                    (1, rank, step * width), lambda place, loop_ref: (loop_ref[0], 0, place)
                ),
            ],
            out_specs=(
                pl.BlockSpec((rows, step * width), lambda place, loop_ref: (0, place)),
                pl.BlockSpec((rows, rank), lambda place, loop_ref: (0, 0)),
                pl.BlockSpec(
                    (LOOP_COUNT, all_rows - rows, step * width),
                    lambda place, loop_ref: (0, 0, place),
                ),
            ),
        ),
        compiler_params=pltpu.CompilerParams(vmem_limit_bytes=48 * 2**20),
    )(loop, arrived, right)


def feed_kernel(normed_ref, cotangent_ref, *refs):
    weights, outs = refs[:-4], refs[-4:]
    hidden_ref, grads_ref, partial_ref, branch_ref = outs
    normed = normed_ref[...]
    cotangent = cotangent_ref[...]
    scale = math.sqrt(2.0 / math.pi)
    partial = None
    for index in range(len(weights) // 2):
        gate_down_ref, up_ref = weights[2 * index : 2 * index + 2]
        width = up_ref.shape[1]
        gate_act = jnp.dot(normed, gate_down_ref[:, :width], preferred_element_type=f32)
        up_act = jnp.dot(normed, up_ref[...], preferred_element_type=f32)
        hidden_grad = jnp.dot(cotangent, gate_down_ref[:, width:], preferred_element_type=f32)
        square = gate_act * gate_act
        tanh_part = jnp.tanh(scale * (gate_act + 0.044715 * (gate_act * square)))
        half_sum = 0.5 * (1.0 + tanh_part)
        gelu = gate_act * half_sum
        slope = half_sum + (0.5 * gate_act) * (1.0 - tanh_part * tanh_part) * (
            scale * (1.0 + (3.0 * 0.044715) * square)
        )
        hidden = (gelu * up_act).astype(bf16)
        gate_grad = (hidden_grad * up_act * slope).astype(bf16)
        up_grad = (hidden_grad * gelu).astype(bf16)
        hidden_ref[:, index * width : (index + 1) * width] = hidden
        grads_ref[:, 2 * index * width : (2 * index + 1) * width] = gate_grad
        grads_ref[:, (2 * index + 1) * width : (2 * index + 2) * width] = up_grad
        sums = [
            lax.dot_general(
                left, right, (((1,), (1,)), ((), ())), preferred_element_type=f32
            )
            for left, right in (
                (gate_grad, gate_down_ref[:, :width]),
                (up_grad, up_ref[...]),
                (hidden, gate_down_ref[:, width:]),
            )
        ]
        if partial is None:
            partial = sums[0] + sums[1]
            branch = sums[2]
        else:
            partial = partial + sums[0] + sums[1]
            branch = branch + sums[2]
    partial_ref[...] = partial
    branch_ref[...] = branch.astype(bf16)


def feed_forward(normed, cotangent, weights):
    rows, model_width = normed.shape
    width = weights[1].shape[1]
    pairs = len(weights) // 2
    tile = math.gcd(rows, 256)
    row_block = pl.BlockSpec((tile, model_width), lambda step: (step, 0))
    return pl.pallas_call(
        feed_kernel,
        out_shape=(
            jax.ShapeDtypeStruct((rows, pairs * width), bf16),
            jax.ShapeDtypeStruct((rows, 2 * pairs * width), bf16),
            jax.ShapeDtypeStruct((rows, model_width), f32),
            jax.ShapeDtypeStruct((rows, model_width), bf16),
        ),
        grid=(rows // tile,),
        in_specs=[row_block, row_block]
        + [
            pl.BlockSpec(
                weight.shape, lambda step: (0, 0), pipeline_mode=pl.Buffered(1)
            )
            for weight in weights
        ],
        out_specs=(
            pl.BlockSpec((tile, pairs * width), lambda step: (step, 0)),
            pl.BlockSpec((tile, 2 * pairs * width), lambda step: (step, 0)),
            row_block,
            row_block,
        ),
        compiler_params=pltpu.CompilerParams(vmem_limit_bytes=56 * 2**20),
    )(normed, cotangent, *weights)


def body(
    tokens,
    cotangent,
    token_sequence_index,
    positions,
    token_exit_loop,
    current_loop,
    attention_norm_gain,
    feedforward_norm_gain,
    probe,
    query_matrix,
    key_value_matrix,
    output_matrix,
    gate_matrix,
    up_matrix,
    down_matrix,
    query_update_left,
    query_update_right,
    key_value_update_left,
    key_value_update_right,
    output_update_left,
    output_update_right,
    gate_update_left,
    gate_update_right,
    up_update_left,
    up_update_right,
    down_update_left,
    down_update_right,
):
    loop_selection = current_loop[0]
    score_scale = HEAD_SIZE ** (-0.5)
    mp_count = lax.axis_size("mp")
    dp_count = lax.axis_size("dp")
    mp_place = lax.axis_index("mp")
    dp_place = lax.axis_index("dp")
    row_count, model_width = tokens.shape
    own_rows = row_count // mp_count
    block_width, query_cols = query_matrix.shape
    head_count = query_cols // HEAD_SIZE
    hidden_own = gate_matrix.shape[1] // dp_count
    rank = gate_update_left.shape[2]
    rank_own = rank // dp_count

    def pick(table):
        return lax.dynamic_index_in_dim(table, loop_selection, 0, keepdims=False)

    q_left, kv_left, o_left = map(
        pick, (query_update_left, key_value_update_left, output_update_left)
    )
    gate_left, up_left, down_left = map(pick, (gate_update_left, up_update_left, down_update_left))
    q_right, kv_right, o_right = map(
        pick, (query_update_right, key_value_update_right, output_update_right)
    )
    def merge(base, left, right, pairs=False):
        return (base.astype(f32) + update_delta(left, right, pairs)).astype(bf16)

    def own_slice(value):
        return lax.dynamic_slice_in_dim(value, mp_place * own_rows, own_rows, 0)

    def to_places(shard, width):
        blocks = [shard[:, place * width : (place + 1) * width] for place in range(dp_count)]
        return jnp.stack(blocks, axis=0)

    block_rows = block_width // mp_count

    def block_slice(value):
        return lax.dynamic_slice_in_dim(value, mp_place * block_rows, block_rows, 0)

    kv_full = lax.all_gather(
        merge(block_slice(key_value_matrix), block_slice(kv_left), kv_right, True),
        ("dp", "mp"),
        axis=0,
        tiled=True,
    )
    q_o_full = lax.all_gather(
        jnp.concatenate(
            [merge(query_matrix, q_left, q_right), merge(output_matrix, o_left, o_right)], axis=1
        ),
        "dp",
        axis=0,
        tiled=True,
    )
    q_full = q_o_full[:, :query_cols]
    o_full = q_o_full[:, query_cols:]

    cotangent_own = own_slice(cotangent)
    cotangent_rows = gather_near(gather_far(cotangent_own))

    tokens_own = own_slice(tokens).astype(f32)
    normed_b = rms_norm(tokens.astype(f32), attention_norm_gain).astype(bf16)

    def send_cols(rows_own):
        return exchange(to_places(rows_own, block_width))

    def all_token_cols(arrived):
        cols = gather_mp(arrived.reshape(-1, block_width))
        cols = cols.reshape(mp_count, dp_count, own_rows, block_width)
        return jnp.swapaxes(cols, 0, 1).reshape(dp_count * row_count, block_width)

    normed_cols = all_token_cols(send_cols(own_slice(normed_b)))
    pair_own = dot(own_slice(normed_b), kv_full)
    seq_own = own_slice(token_sequence_index)
    spots_own = own_slice(positions)
    marks = jnp.stack([seq_own, spots_own // 64, spots_own % 64], axis=0).astype(bf16)
    marks = jnp.pad(marks, ((0, 5), (0, 2 * HEAD_SIZE - own_rows)))
    outgoing = jnp.concatenate(
        [
            rotate(pair_own[:, :HEAD_SIZE], spots_own, 1.0).astype(bf16),
            pair_own[:, HEAD_SIZE:].astype(bf16),
        ],
        axis=1,
    )
    outgoing = jnp.concatenate([outgoing, marks], axis=0)
    pairs_far = after(gather_far(outgoing), *halves(cotangent_rows))
    pairs_front = gather_near(pairs_far)
    all_pairs = jnp.concatenate([pairs_front, other_core(pairs_front)], axis=0)
    all_pairs = all_pairs.reshape(-1, own_rows + 8, 2 * HEAD_SIZE)
    all_keys = all_pairs[:, :own_rows, :HEAD_SIZE].reshape(-1, HEAD_SIZE)
    all_values = all_pairs[:, :own_rows, HEAD_SIZE:].reshape(-1, HEAD_SIZE)
    all_marks = all_pairs[:, own_rows : own_rows + 3, :own_rows].astype(jnp.int32)
    all_seq = all_marks[:, 0].reshape(-1)
    all_spots = (all_marks[:, 1] * 64 + all_marks[:, 2]).reshape(-1)
    queries = dot(normed_b, q_full)
    query_b = rotate(queries.reshape(row_count, head_count, HEAD_SIZE), positions, 1.0).astype(
        bf16
    )
    gate_down = exchange(
        merge_blocks(
            after(current_loop, *halves(pairs_front)),
            dp_count,
            [
                (gate_matrix, gate_update_left, gate_update_right),
                (down_matrix, down_update_left, down_update_right),
            ],
        )
    ).reshape(model_width, 2 * hidden_own)
    query_b = after(query_b, normed_cols)
    weights_soft = attention_weights(
        query_b, all_keys, token_sequence_index, positions, all_seq, all_spots, score_scale
    )
    weights_low = weights_soft.astype(bf16)
    attended = jnp.einsum("hqk,kd->qhd", weights_low, all_values, preferred_element_type=f32)
    attended_b = attended.reshape(row_count, query_cols).astype(bf16)
    middle = tokens_own + scatter_mp(dot_cols(attended_b, o_full))
    normed2_b = rms_norm(middle, feedforward_norm_gain).astype(bf16)

    normed2_far = gather_far(after(normed2_b, gate_down))
    up_own = exchange(
        merge_blocks(
            after(current_loop, normed2_far),
            dp_count,
            [(up_matrix, up_update_left, up_update_right)],
        )
    ).reshape(model_width, hidden_own)
    normed2_rows = gather_near(normed2_far)
    left_block = jnp.concatenate([gate_left, up_left, down_left], axis=1)
    left_all = lax.all_gather(
        after(block_slice(left_block), gate_down), ("dp", "mp"), axis=0, tiled=True
    )
    attended_late = after(lax.optimization_barrier(attended_b), left_all)
    attended_all = lax.all_gather(attended_late, "dp", axis=0, tiled=True)
    gate_down_other = swap(gate_down, "mp", 1)
    up_other = swap(after(up_own, *halves(normed2_rows)), "mp", 1)
    hidden_b, unit_grad_b, partial, branch_part = feed_forward(
        normed2_rows, cotangent_rows, (gate_down, up_own, gate_down_other, up_other)
    )
    normed2_near = scatter_near(partial)

    def weight_grad(rows, grads, width):
        sent = dot_rows(rows, grads[:, width:]).astype(bf16)
        kept = dot_rows(rows, grads[:, :width])
        return (kept + swap(sent, "mp", 1).astype(f32)).astype(bf16)

    def to_blocks(grad_b, left_cols):
        right_part = dot_rows(left_cols, grad_b).astype(bf16)
        return [
            grad_b.reshape(dp_count, block_width, hidden_own),
            right_part.reshape(dp_count, rank_own, hidden_own),
        ]

    down_grad_b = weight_grad(cotangent_rows, hidden_b, hidden_own)
    gate_up_grad_b = weight_grad(normed2_rows, unit_grad_b, 2 * hidden_own)
    down_sent = exchange(
        jnp.concatenate(to_blocks(down_grad_b, after(left_all[:, 2 * rank :], attended_all)), axis=1)
    )
    gate_up_blocks = jnp.concatenate(
        to_blocks(gate_up_grad_b[:, :hidden_own], left_all[:, :rank])
        + to_blocks(gate_up_grad_b[:, hidden_own:], left_all[:, rank : 2 * rank]),
        axis=1,
    )
    normed2_grad = scatter_far(after(normed2_near, down_sent, gate_up_blocks))

    unused_norm, mlp_pull = jax.vjp(rms_norm, middle, feedforward_norm_gain)
    middle_norm_grad, mlp_gain_part = mlp_pull(normed2_grad)
    middle_grad = cotangent_own.astype(f32) + middle_norm_grad
    branch_grad_own = middle_grad.astype(bf16)
    branch_sent = send_cols(branch_grad_own)
    gate_up_sent = exchange(after(gate_up_blocks, branch_sent))
    branch_grad = gather_mp(branch_grad_own).reshape(row_count, model_width)
    attended_grad_b = (
        dot(branch_grad, o_full).astype(bf16).reshape(row_count, head_count, HEAD_SIZE)
    )
    prob_grad = jnp.einsum("qhd,kd->hqk", attended_grad_b, all_values, preferred_element_type=f32)
    score_grad_b = (
        weights_soft * (prob_grad - jnp.sum(prob_grad * weights_soft, axis=-1, keepdims=True))
    ).astype(bf16)
    keys_grad = (
        jnp.einsum("hqk,qhd->kd", score_grad_b, query_b, preferred_element_type=f32) * score_scale
    )
    values_grad = jnp.einsum(
        "hqk,qhd->kd", weights_low, attended_grad_b, preferred_element_type=f32
    )
    pair_partial = jnp.concatenate([keys_grad, values_grad], axis=1)
    half = pair_partial.shape[0] // 2
    block_all = block_width + rank_own

    down_weight_grad, down_lora_a, down_lora_b = receive_grad(
        after(current_loop, attended_grad_b), down_sent, 0, block_all, down_update_right, block_width
    )
    pair_near = scatter_near(add_core(pair_partial[half:], pair_partial[:half]))
    branch_near = scatter_near(after(branch_part, attended_grad_b))
    query_grad = (
        jnp.einsum("hqk,kd->qhd", score_grad_b, all_keys, preferred_element_type=f32) * score_scale
    )
    query_grad_b = rotate(query_grad, positions, -1.0).reshape(row_count, query_cols).astype(bf16)
    query_grad_all = lax.all_gather(query_grad_b, "dp", axis=0, tiled=True)
    pair_grad_own = scatter_far(after(pair_near, gate_up_sent))
    branch_cols = all_token_cols(branch_sent)
    q_weight_grad = dot_rows(after(normed_cols, pair_grad_own), query_grad_all)
    o_weight_grad = dot_rows(branch_cols, attended_all)
    q_weight_b = q_weight_grad.astype(bf16)
    o_weight_b = o_weight_grad.astype(bf16)
    qo_lora_a = sum_mp(
        jnp.concatenate([dot_cols(q_weight_b, q_right), dot_cols(o_weight_b, o_right)], axis=1)
    )
    qo_right = jnp.concatenate(
        [dot_rows(q_left, q_weight_b), dot_rows(o_left, o_weight_b)], axis=1
    ).astype(bf16)
    pair_grad_b = jnp.concatenate(
        [rotate(pair_grad_own[:, :HEAD_SIZE], spots_own, -1.0), pair_grad_own[:, HEAD_SIZE:]],
        axis=1,
    ).astype(bf16)
    mlp_branch = scatter_far(after(branch_near, pair_grad_own))
    output_rows = middle + mlp_branch
    mixed = gather_mp(output_rows.astype(bf16)).reshape(row_count, model_width)
    confidence_own = jnp.sum(jax.nn.sigmoid(jnp.dot(output_rows, probe, precision=precise)))
    levels = jnp.arange(LOOP_COUNT, dtype=jnp.int32)
    exit_own = own_slice(token_exit_loop)
    depth_own = jnp.sum((exit_own[:, None] == levels[None, :]).astype(f32), axis=0)

    normed_grad = scatter_mp(dot_cols(query_grad_b, q_full)) + dot_cols(pair_grad_b, kv_full)
    unused_first, attn_pull = jax.vjp(rms_norm, tokens_own, attention_norm_gain)
    inputs_norm_grad, attn_gain_part = attn_pull(normed_grad)
    tokens_grad = gather_mp(middle_grad + inputs_norm_grad).reshape(row_count, model_width)

    pair_grad_all = lax.all_gather(pair_grad_b, ("dp", "mp"), axis=0, tiled=True)
    small = sum_all(
        jnp.concatenate([attn_gain_part, mlp_gain_part, depth_own, confidence_own.reshape(1)])
    )
    kv_weight_grad = dot_rows(normed_cols, after(pair_grad_all, small))
    kv_weight_b = kv_weight_grad.astype(bf16)
    kv_lora_a = jnp.concatenate(
        [
            dot_cols(kv_weight_b[:, :HEAD_SIZE], kv_right[:, :HEAD_SIZE]),
            dot_cols(kv_weight_b[:, HEAD_SIZE:], kv_right[:, HEAD_SIZE:]),
        ],
        axis=1,
    )
    right_parts = jnp.concatenate(
        [
            qo_right,
            dot_rows(kv_left[:, :rank], kv_weight_b[:, :HEAD_SIZE]).astype(bf16),
            dot_rows(kv_left[:, rank:], kv_weight_b[:, HEAD_SIZE:]).astype(bf16),
        ],
        axis=1,
    )
    right_grads = jnp.sum(
        exchange(right_parts.reshape(dp_count, rank_own, -1)).astype(f32), axis=0
    )

    late_loop = after(current_loop, pair_grad_own)
    gate_weight_grad, gate_lora_a, gate_lora_b = receive_grad(
        late_loop, gate_up_sent, 0, block_all, gate_update_right, block_width
    )
    up_weight_grad, up_lora_a, up_lora_b = receive_grad(
        late_loop, gate_up_sent, 1, block_all, up_update_right, block_width
    )
    mlp_lora_a = sum_mp(jnp.concatenate([gate_lora_a, up_lora_a, down_lora_a], axis=1))

    gain_width = model_width // dp_count
    attn_gain_grad = lax.dynamic_slice_in_dim(small, dp_place * gain_width, gain_width, 0)
    mlp_gain_grad = lax.dynamic_slice_in_dim(
        small, model_width + dp_place * gain_width, gain_width, 0
    )
    counts = small[2 * model_width : 2 * model_width + LOOP_COUNT].astype(jnp.int32)
    confidence = small[2 * model_width + LOOP_COUNT :] / (row_count * dp_count)

    def place_loop(grad_item):
        chosen = jnp.arange(LOOP_COUNT)[:, None, None] == loop_selection
        return jnp.where(chosen, grad_item[None], 0.0)

    return (
        counts,
        confidence,
        mixed,
        tokens_grad,
        attn_gain_grad,
        mlp_gain_grad,
        q_weight_grad,
        kv_weight_grad,
        o_weight_grad,
        gate_weight_grad,
        up_weight_grad,
        down_weight_grad,
        place_loop(qo_lora_a[:, :rank]),
        place_loop(right_grads[:, :query_cols]),
        place_loop(kv_lora_a),
        place_loop(right_grads[:, 2 * query_cols :]),
        place_loop(qo_lora_a[:, rank:]),
        place_loop(right_grads[:, query_cols : 2 * query_cols]),
        place_loop(mlp_lora_a[:, :rank]),
        gate_lora_b,
        place_loop(mlp_lora_a[:, rank : 2 * rank]),
        up_lora_b,
        place_loop(mlp_lora_a[:, 2 * rank :]),
        down_lora_b,
    )


def solution(mesh):
    return jax.shard_map(
        body,
        mesh=mesh,
        in_specs=(
            P("dp", None),
            P("dp", None),
            P("dp"),
            P("dp"),
            P("dp"),
            P(),
            P(),
            P(),
            P(),
            P("dp", "mp"),
            P("dp", None),
            P("dp", "mp"),
            P("dp", "mp"),
            P("dp", "mp"),
            P("dp", "mp"),
            P(None, "dp", None),
            P(None, None, "mp"),
            P(None, "dp", None),
            P(),
            P(None, "dp", None),
            P(None, None, "mp"),
            P(None, "dp", None),
            P(None, None, "mp"),
            P(None, "dp", None),
            P(None, None, "mp"),
            P(None, "dp", None),
            P(None, None, "mp"),
        ),
        out_specs=(
            P(),
            P(),
            P("dp", None),
            P("dp", None),
            P("dp"),
            P("dp"),
            P("dp", "mp"),
            P("dp", None),
            P("dp", "mp"),
            P("dp", "mp"),
            P("dp", "mp"),
            P("dp", "mp"),
            P(None, "dp", None),
            P(None, "dp", "mp"),
            P(None, "dp", None),
            P(None, "dp", None),
            P(None, "dp", None),
            P(None, "dp", "mp"),
            P(None, "dp", None),
            P(None, "dp", "mp"),
            P(None, "dp", None),
            P(None, "dp", "mp"),
            P(None, "dp", None),
            P(None, "dp", "mp"),
        ),
        check_vma=False,
    )
```

```python
import math

import jax
import jax.numpy as jnp
from jax import lax
from jax.experimental import pallas as pl
from jax.experimental.pallas import tpu as pltpu
from jax.sharding import PartitionSpec as P

HEAD_SIZE = 256
LOOP_COUNT = 3


EPSILON = 1e-06
MASKED_SCORE = -1e30
precise = lax.Precision.HIGHEST
f32 = jnp.float32
bf16 = jnp.bfloat16


def rms_norm(inputs, gain):
    return inputs * lax.rsqrt(jnp.mean(inputs * inputs, axis=-1, keepdims=True) + EPSILON) * gain


def rotate(inputs, spots, direction):
    half_width = inputs.shape[-1] // 2
    frequency = jnp.exp(
        jnp.arange(half_width, dtype=jnp.float32) * (-2.0 * math.log(10000.0) / inputs.shape[-1])
    )
    angles = spots.astype(jnp.float32)[:, None] * frequency[None, :]
    cos_part = jnp.cos(angles)
    sin_part = jnp.sin(angles) * direction
    if inputs.ndim == 3:
        cos_part = cos_part[:, None, :]
        sin_part = sin_part[:, None, :]
    first_half = inputs[..., :half_width]
    second_half = inputs[..., half_width:]
    return jnp.concatenate(
        [
            first_half * cos_part - second_half * sin_part,
            second_half * cos_part + first_half * sin_part,
        ],
        axis=-1,
    )


def update_delta(left_factor, right_factor, factor_pairs):
    if factor_pairs:
        rank_half = left_factor.shape[1] // 2
        width_half = right_factor.shape[1] // 2
        key_half = jnp.dot(
            left_factor[:, :rank_half],
            right_factor[:, :width_half],
            preferred_element_type=jnp.float32,
        )
        value_half = jnp.dot(
            left_factor[:, rank_half:],
            right_factor[:, width_half:],
            preferred_element_type=jnp.float32,
        )
        return jnp.concatenate([key_half, value_half], axis=1)
    return jnp.dot(left_factor, right_factor, preferred_element_type=jnp.float32)


def attention_weights(queries, key_rows, query_seq, query_spots, key_seq, key_spots, score_scale):
    scores = (
        jnp.einsum("qhd,kd->hqk", queries, key_rows, preferred_element_type=jnp.float32)
        * score_scale
    )
    allowed = (query_seq[:, None] == key_seq[None, :]) & (
        key_spots[None, :] <= query_spots[:, None]
    )
    scores = jnp.where(allowed[None], scores, MASKED_SCORE)
    return jax.nn.softmax(scores, axis=-1)


def dot(left, right):
    return jnp.dot(left, right, preferred_element_type=f32)


def dot_rows(left, right):
    return lax.dot_general(left, right, (((0,), (0,)), ((), ())), preferred_element_type=f32)


def dot_cols(left, right):
    return lax.dot_general(left, right, (((1,), (1,)), ((), ())), preferred_element_type=f32)


def swap(value, axis, bit):
    count = lax.axis_size(axis)
    return lax.ppermute(value, axis, [(place, place ^ bit) for place in range(count)])


def exchange(blocks):
    return lax.all_to_all(blocks, "dp", 0, 0, tiled=True)


def far_bits():
    bit = lax.axis_size("dp") // 2
    bits = []
    while bit > 1:
        bits.append(bit)
        bit = bit // 2
    return bits


def grow(value, axis, bit):
    return jnp.concatenate([value, swap(value, axis, bit)], axis=0)


def fold(value, axis, bit):
    half = value.shape[0] // 2
    arrived = swap(value[half:].astype(bf16), axis, bit)
    return value[:half] + arrived.astype(f32)


def after(value, *others):
    total = jnp.zeros((), f32)
    for other in others:
        last = other[tuple(size - 1 for size in other.shape)]
        total = jnp.maximum(total, jnp.abs(last.astype(f32)))
    return value + jnp.minimum(total, 0.0).astype(value.dtype)


def halves(value):
    half = value.shape[0] // 2
    return value[:half], value[half:]


def gather_mp(value):
    place = lax.axis_index("mp")
    arrived = swap(value, "mp", 2)
    value = jnp.where(
        place < 2, jnp.stack([value, arrived], axis=0), jnp.stack([arrived, value], axis=0)
    )
    arrived = swap(value, "mp", 1)
    return jnp.where(
        place % 2 == 0, jnp.stack([value, arrived], axis=1), jnp.stack([arrived, value], axis=1)
    )


def scatter_mp(value):
    place = lax.axis_index("mp")
    for axis, bit, own in ((1, 1, place % 2), (0, 2, place // 2)):
        if axis == 1:
            value = value.reshape((2, 2, value.shape[0] // 4) + value.shape[1:])
        sent = lax.dynamic_index_in_dim(value, 1 - own, axis, keepdims=False)
        kept = lax.dynamic_index_in_dim(value, own, axis, keepdims=False)
        value = kept + swap(sent.astype(bf16), "mp", bit).astype(f32)
    return value


def gather_far(value):
    for bit in far_bits():
        value = grow(value, "dp", bit)
    return value


def gather_near(value):
    half = value.shape[0] // 2
    front = grow(grow(value[:half], "dp", 1), "mp", 2)
    rear = grow(grow(value[half:], "mp", 2), "dp", 1)
    return jnp.concatenate([front, rear], axis=0)


def other_core(value):
    return swap(value, "mp", 1)


def add_core(sent, kept):
    return kept + swap(sent.astype(bf16), "mp", 1).astype(f32)


def scatter_near(value):
    value = value.astype(f32)
    half = value.shape[0] // 2
    front = fold(fold(value[:half], "mp", 2), "dp", 1)
    rear = fold(fold(value[half:], "dp", 1), "mp", 2)
    return jnp.concatenate([front, rear], axis=0)


def scatter_far(value):
    for bit in reversed(far_bits()):
        value = fold(value, "dp", bit)
    return value


def sum_all(value):
    for axis in ("mp", "dp"):
        bit = 1
        while bit < lax.axis_size(axis):
            value = value + swap(value, axis, bit)
            bit = bit * 2
    return value


def sum_mp(value):
    value = value + swap(value, "mp", 1)
    low = value.astype(bf16)
    return low.astype(f32) + swap(low, "mp", 2).astype(f32)


def merge_kernel(loop_ref, *refs):
    out_ref = refs[-1]
    width = refs[0].shape[1]
    for index in range(len(refs) // 3):
        base_ref, left_ref, right_ref = refs[3 * index : 3 * index + 3]
        delta = jnp.dot(left_ref[0], right_ref[0], preferred_element_type=f32)
        merged = base_ref[...].astype(f32) + delta
        out_ref[0, :, index * width : (index + 1) * width] = merged.astype(bf16)


def merge_blocks(loop, places, weights):
    rows, columns = weights[0][0].shape
    rank = weights[0][1].shape[2]
    width = columns // places
    specs = []
    arrays = []
    for base, left, right in weights:
        specs.append(pl.BlockSpec((rows, width), lambda place, loop_ref: (0, place)))
        specs.append(pl.BlockSpec((1, rows, rank), lambda place, loop_ref: (loop_ref[0], 0, 0)))
        specs.append(
            pl.BlockSpec((1, rank, width), lambda place, loop_ref: (loop_ref[0], 0, place))
        )
        arrays += [base, left, right]
    return pl.pallas_call(
        merge_kernel,
        out_shape=jax.ShapeDtypeStruct((places, rows, width * len(weights)), bf16),
        grid_spec=pltpu.PrefetchScalarGridSpec(
            num_scalar_prefetch=1,
            grid=(places,),
            in_specs=specs,
            out_specs=pl.BlockSpec(
                (1, rows, width * len(weights)), lambda place, loop_ref: (place, 0, 0)
            ),
        ),
        compiler_params=pltpu.CompilerParams(vmem_limit_bytes=48 * 2**20),
    )(loop, *arrays)


def receive_kernel(loop_ref, arrived_ref, right_ref, grad_ref, left_grad_ref, right_grad_ref):
    rows = grad_ref.shape[0]
    width = arrived_ref.shape[2]
    total = None
    for place in range(arrived_ref.shape[0]):
        columns = slice(place * width, (place + 1) * width)
        block = arrived_ref[place, :rows, :]
        grad_ref[:, columns] = block.astype(f32)
        part = lax.dot_general(
            block, right_ref[0, :, columns], (((1,), (1,)), ((), ())), preferred_element_type=f32
        )
        total = part if total is None else total + part
        right_grad = arrived_ref[place, rows:, :].astype(f32)
        for loop in range(LOOP_COUNT):
            right_grad_ref[loop, :, columns] = jnp.where(loop_ref[0] == loop, right_grad, 0.0)

    @pl.when(pl.program_id(0) == 0)
    def first():
        left_grad_ref[...] = total

    @pl.when(pl.program_id(0) > 0)
    def later():
        left_grad_ref[...] += total


def receive_grad(loop, arrived, which, all_rows, right, rows):
    places, _, width = arrived.shape
    rank = right.shape[1]
    step = 2
    return pl.pallas_call(
        receive_kernel,
        out_shape=(
            jax.ShapeDtypeStruct((rows, places * width), f32),
            jax.ShapeDtypeStruct((rows, rank), f32),
            jax.ShapeDtypeStruct((LOOP_COUNT, all_rows - rows, places * width), f32),
        ),
        grid_spec=pltpu.PrefetchScalarGridSpec(
            num_scalar_prefetch=1,
            grid=(places // step,),
            in_specs=[
                pl.BlockSpec((step, all_rows, width), lambda place, loop_ref: (place, which, 0)),
                pl.BlockSpec(
                    (1, rank, step * width), lambda place, loop_ref: (loop_ref[0], 0, place)
                ),
            ],
            out_specs=(
                pl.BlockSpec((rows, step * width), lambda place, loop_ref: (0, place)),
                pl.BlockSpec((rows, rank), lambda place, loop_ref: (0, 0)),
                pl.BlockSpec(
                    (LOOP_COUNT, all_rows - rows, step * width),
                    lambda place, loop_ref: (0, 0, place),
                ),
            ),
        ),
        compiler_params=pltpu.CompilerParams(vmem_limit_bytes=48 * 2**20),
    )(loop, arrived, right)


def feed_kernel(normed_ref, cotangent_ref, *refs):
    weights, outs = refs[:-4], refs[-4:]
    hidden_ref, grads_ref, partial_ref, branch_ref = outs
    normed = normed_ref[...]
    cotangent = cotangent_ref[...]
    scale = math.sqrt(2.0 / math.pi)
    partial = None
    for index in range(len(weights) // 2):
        gate_down_ref, up_ref = weights[2 * index : 2 * index + 2]
        width = up_ref.shape[1]
        gate_act = jnp.dot(normed, gate_down_ref[:, :width], preferred_element_type=f32)
        up_act = jnp.dot(normed, up_ref[...], preferred_element_type=f32)
        hidden_grad = jnp.dot(cotangent, gate_down_ref[:, width:], preferred_element_type=f32)
        square = gate_act * gate_act
        tanh_part = jnp.tanh(scale * (gate_act + 0.044715 * (gate_act * square)))
        half_sum = 0.5 * (1.0 + tanh_part)
        gelu = gate_act * half_sum
        slope = half_sum + (0.5 * gate_act) * (1.0 - tanh_part * tanh_part) * (
            scale * (1.0 + (3.0 * 0.044715) * square)
        )
        hidden = (gelu * up_act).astype(bf16)
        gate_grad = (hidden_grad * up_act * slope).astype(bf16)
        up_grad = (hidden_grad * gelu).astype(bf16)
        hidden_ref[:, index * width : (index + 1) * width] = hidden
        grads_ref[:, 2 * index * width : (2 * index + 1) * width] = gate_grad
        grads_ref[:, (2 * index + 1) * width : (2 * index + 2) * width] = up_grad
        sums = [
            lax.dot_general(
                left, right, (((1,), (1,)), ((), ())), preferred_element_type=f32
            )
            for left, right in (
                (gate_grad, gate_down_ref[:, :width]),
                (up_grad, up_ref[...]),
                (hidden, gate_down_ref[:, width:]),
            )
        ]
        if partial is None:
            partial = sums[0] + sums[1]
            branch = sums[2]
        else:
            partial = partial + sums[0] + sums[1]
            branch = branch + sums[2]
    partial_ref[...] = partial
    branch_ref[...] = branch.astype(bf16)


def feed_forward(normed, cotangent, weights):
    rows, model_width = normed.shape
    width = weights[1].shape[1]
    pairs = len(weights) // 2
    tile = math.gcd(rows, 256)
    row_block = pl.BlockSpec((tile, model_width), lambda step: (step, 0))
    return pl.pallas_call(
        feed_kernel,
        out_shape=(
            jax.ShapeDtypeStruct((rows, pairs * width), bf16),
            jax.ShapeDtypeStruct((rows, 2 * pairs * width), bf16),
            jax.ShapeDtypeStruct((rows, model_width), f32),
            jax.ShapeDtypeStruct((rows, model_width), bf16),
        ),
        grid=(rows // tile,),
        in_specs=[row_block, row_block]
        + [
            pl.BlockSpec(
                weight.shape, lambda step: (0, 0), pipeline_mode=pl.Buffered(1)
            )
            for weight in weights
        ],
        out_specs=(
            pl.BlockSpec((tile, pairs * width), lambda step: (step, 0)),
            pl.BlockSpec((tile, 2 * pairs * width), lambda step: (step, 0)),
            row_block,
            row_block,
        ),
        compiler_params=pltpu.CompilerParams(vmem_limit_bytes=56 * 2**20),
    )(normed, cotangent, *weights)


def body(
    tokens,
    cotangent,
    token_sequence_index,
    positions,
    token_exit_loop,
    current_loop,
    attention_norm_gain,
    feedforward_norm_gain,
    probe,
    query_matrix,
    key_value_matrix,
    output_matrix,
    gate_matrix,
    up_matrix,
    down_matrix,
    query_update_left,
    query_update_right,
    key_value_update_left,
    key_value_update_right,
    output_update_left,
    output_update_right,
    gate_update_left,
    gate_update_right,
    up_update_left,
    up_update_right,
    down_update_left,
    down_update_right,
):
    loop_selection = current_loop[0]
    score_scale = HEAD_SIZE ** (-0.5)
    mp_count = lax.axis_size("mp")
    dp_count = lax.axis_size("dp")
    mp_place = lax.axis_index("mp")
    dp_place = lax.axis_index("dp")
    row_count, model_width = tokens.shape
    own_rows = row_count // mp_count
    block_width, query_cols = query_matrix.shape
    head_count = query_cols // HEAD_SIZE
    hidden_own = gate_matrix.shape[1] // dp_count
    rank = gate_update_left.shape[2]
    rank_own = rank // dp_count

    def pick(table):
        return lax.dynamic_index_in_dim(table, loop_selection, 0, keepdims=False)

    q_left, kv_left, o_left = map(
        pick, (query_update_left, key_value_update_left, output_update_left)
    )
    gate_left, up_left, down_left = map(pick, (gate_update_left, up_update_left, down_update_left))
    q_right, kv_right, o_right = map(
        pick, (query_update_right, key_value_update_right, output_update_right)
    )
    def merge(base, left, right, pairs=False):
        return (base.astype(f32) + update_delta(left, right, pairs)).astype(bf16)

    def own_slice(value):
        return lax.dynamic_slice_in_dim(value, mp_place * own_rows, own_rows, 0)

    def to_places(shard, width):
        blocks = [shard[:, place * width : (place + 1) * width] for place in range(dp_count)]
        return jnp.stack(blocks, axis=0)

    block_rows = block_width // mp_count

    def block_slice(value):
        return lax.dynamic_slice_in_dim(value, mp_place * block_rows, block_rows, 0)

    kv_full = lax.all_gather(
        merge(block_slice(key_value_matrix), block_slice(kv_left), kv_right, True),
        ("dp", "mp"),
        axis=0,
        tiled=True,
    )
    q_o_full = lax.all_gather(
        jnp.concatenate(
            [merge(query_matrix, q_left, q_right), merge(output_matrix, o_left, o_right)], axis=1
        ),
        "dp",
        axis=0,
        tiled=True,
    )
    q_full = q_o_full[:, :query_cols]
    o_full = q_o_full[:, query_cols:]

    cotangent_own = own_slice(cotangent)
    cotangent_rows = gather_near(gather_far(cotangent_own))

    tokens_own = own_slice(tokens).astype(f32)
    normed_b = rms_norm(tokens.astype(f32), attention_norm_gain).astype(bf16)

    def send_cols(rows_own):
        return exchange(to_places(rows_own, block_width))

    def all_token_cols(arrived):
        cols = gather_mp(arrived.reshape(-1, block_width))
        cols = cols.reshape(mp_count, dp_count, own_rows, block_width)
        return jnp.swapaxes(cols, 0, 1).reshape(dp_count * row_count, block_width)

    normed_cols = all_token_cols(send_cols(own_slice(normed_b)))
    pair_own = dot(own_slice(normed_b), kv_full)
    seq_own = own_slice(token_sequence_index)
    spots_own = own_slice(positions)
    marks = jnp.stack([seq_own, spots_own // 64, spots_own % 64], axis=0).astype(bf16)
    marks = jnp.pad(marks, ((0, 5), (0, 2 * HEAD_SIZE - own_rows)))
    outgoing = jnp.concatenate(
        [
            rotate(pair_own[:, :HEAD_SIZE], spots_own, 1.0).astype(bf16),
            pair_own[:, HEAD_SIZE:].astype(bf16),
        ],
        axis=1,
    )
    outgoing = jnp.concatenate([outgoing, marks], axis=0)
    pairs_far = after(gather_far(outgoing), *halves(cotangent_rows))
    pairs_front = gather_near(pairs_far)
    all_pairs = jnp.concatenate([pairs_front, other_core(pairs_front)], axis=0)
    all_pairs = all_pairs.reshape(-1, own_rows + 8, 2 * HEAD_SIZE)
    all_keys = all_pairs[:, :own_rows, :HEAD_SIZE].reshape(-1, HEAD_SIZE)
    all_values = all_pairs[:, :own_rows, HEAD_SIZE:].reshape(-1, HEAD_SIZE)
    all_marks = all_pairs[:, own_rows : own_rows + 3, :own_rows].astype(jnp.int32)
    all_seq = all_marks[:, 0].reshape(-1)
    all_spots = (all_marks[:, 1] * 64 + all_marks[:, 2]).reshape(-1)
    queries = dot(normed_b, q_full)
    query_b = rotate(queries.reshape(row_count, head_count, HEAD_SIZE), positions, 1.0).astype(
        bf16
    )
    gate_down = exchange(
        merge_blocks(
            after(current_loop, *halves(pairs_front)),
            dp_count,
            [
                (gate_matrix, gate_update_left, gate_update_right),
                (down_matrix, down_update_left, down_update_right),
            ],
        )
    ).reshape(model_width, 2 * hidden_own)
    query_b = after(query_b, normed_cols)
    weights_soft = attention_weights(
        query_b, all_keys, token_sequence_index, positions, all_seq, all_spots, score_scale
    )
    weights_low = weights_soft.astype(bf16)
    attended = jnp.einsum("hqk,kd->qhd", weights_low, all_values, preferred_element_type=f32)
    attended_b = attended.reshape(row_count, query_cols).astype(bf16)
    middle = tokens_own + scatter_mp(dot_cols(attended_b, o_full))
    normed2_b = rms_norm(middle, feedforward_norm_gain).astype(bf16)

    cotangent_rows = lax.optimization_barrier(cotangent_rows)
    normed2_far = gather_far(after(normed2_b, gate_down, cotangent_rows))
    up_own = exchange(
        merge_blocks(
            after(current_loop, normed2_far),
            dp_count,
            [(up_matrix, up_update_left, up_update_right)],
        )
    ).reshape(model_width, hidden_own)
    normed2_rows = gather_near(normed2_far)
    left_block = jnp.concatenate([gate_left, up_left, down_left], axis=1)
    left_all = lax.all_gather(
        after(block_slice(left_block), gate_down), ("dp", "mp"), axis=0, tiled=True
    )
    attended_late = after(lax.optimization_barrier(attended_b), left_all)
    attended_all = lax.all_gather(attended_late, "dp", axis=0, tiled=True)
    gate_down_other = swap(gate_down, "mp", 1)
    up_other = swap(after(up_own, *halves(normed2_rows)), "mp", 1)
    hidden_b, unit_grad_b, partial, branch_part = feed_forward(
        normed2_rows, cotangent_rows, (gate_down, up_own, gate_down_other, up_other)
    )
    normed2_near = scatter_near(partial)

    def weight_grad(rows, grads, width):
        sent = dot_rows(rows, grads[:, width:]).astype(bf16)
        kept = dot_rows(rows, grads[:, :width])
        return (kept + swap(sent, "mp", 1).astype(f32)).astype(bf16)

    def to_blocks(grad_b, left_cols):
        right_part = dot_rows(left_cols, grad_b).astype(bf16)
        return [
            grad_b.reshape(dp_count, block_width, hidden_own),
            right_part.reshape(dp_count, rank_own, hidden_own),
        ]

    down_grad_b = weight_grad(cotangent_rows, hidden_b, hidden_own)
    gate_up_grad_b = weight_grad(normed2_rows, unit_grad_b, 2 * hidden_own)
    down_sent = exchange(
        jnp.concatenate(to_blocks(down_grad_b, after(left_all[:, 2 * rank :], attended_all)), axis=1)
    )
    gate_up_blocks = jnp.concatenate(
        to_blocks(gate_up_grad_b[:, :hidden_own], left_all[:, :rank])
        + to_blocks(gate_up_grad_b[:, hidden_own:], left_all[:, rank : 2 * rank]),
        axis=1,
    )
    normed2_grad = scatter_far(after(normed2_near, down_sent, gate_up_blocks))

    unused_norm, mlp_pull = jax.vjp(rms_norm, middle, feedforward_norm_gain)
    middle_norm_grad, mlp_gain_part = mlp_pull(normed2_grad)
    middle_grad = cotangent_own.astype(f32) + middle_norm_grad
    branch_grad_own = middle_grad.astype(bf16)
    branch_sent = send_cols(branch_grad_own)
    gate_up_sent = exchange(after(gate_up_blocks, branch_sent))
    branch_grad = gather_mp(branch_grad_own).reshape(row_count, model_width)
    attended_grad_b = (
        dot(branch_grad, o_full).astype(bf16).reshape(row_count, head_count, HEAD_SIZE)
    )
    prob_grad = jnp.einsum("qhd,kd->hqk", attended_grad_b, all_values, preferred_element_type=f32)
    score_grad_b = (
        weights_soft * (prob_grad - jnp.sum(prob_grad * weights_soft, axis=-1, keepdims=True))
    ).astype(bf16)
    keys_grad = (
        jnp.einsum("hqk,qhd->kd", score_grad_b, query_b, preferred_element_type=f32) * score_scale
    )
    values_grad = jnp.einsum(
        "hqk,qhd->kd", weights_low, attended_grad_b, preferred_element_type=f32
    )
    pair_partial = jnp.concatenate([keys_grad, values_grad], axis=1)
    half = pair_partial.shape[0] // 2
    block_all = block_width + rank_own

    down_weight_grad, down_lora_a, down_lora_b = receive_grad(
        after(current_loop, attended_grad_b), down_sent, 0, block_all, down_update_right, block_width
    )
    pair_near = scatter_near(add_core(pair_partial[half:], pair_partial[:half]))
    branch_near = scatter_near(after(branch_part, attended_grad_b))
    query_grad = (
        jnp.einsum("hqk,kd->qhd", score_grad_b, all_keys, preferred_element_type=f32) * score_scale
    )
    query_grad_b = rotate(query_grad, positions, -1.0).reshape(row_count, query_cols).astype(bf16)
    query_grad_all = lax.all_gather(query_grad_b, "dp", axis=0, tiled=True)
    pair_grad_own = scatter_far(after(pair_near, gate_up_sent))
    branch_cols = all_token_cols(branch_sent)
    q_weight_grad = dot_rows(after(normed_cols, pair_grad_own), query_grad_all)
    o_weight_grad = dot_rows(branch_cols, attended_all)
    q_weight_b = q_weight_grad.astype(bf16)
    o_weight_b = o_weight_grad.astype(bf16)
    qo_lora_a = sum_mp(
        jnp.concatenate([dot_cols(q_weight_b, q_right), dot_cols(o_weight_b, o_right)], axis=1)
    )
    qo_right = jnp.concatenate(
        [dot_rows(q_left, q_weight_b), dot_rows(o_left, o_weight_b)], axis=1
    ).astype(bf16)
    pair_grad_b = jnp.concatenate(
        [rotate(pair_grad_own[:, :HEAD_SIZE], spots_own, -1.0), pair_grad_own[:, HEAD_SIZE:]],
        axis=1,
    ).astype(bf16)
    mlp_branch = scatter_far(after(branch_near, pair_grad_own))
    output_rows = middle + mlp_branch
    mixed = gather_mp(output_rows.astype(bf16)).reshape(row_count, model_width)
    confidence_own = jnp.sum(jax.nn.sigmoid(jnp.dot(output_rows, probe, precision=precise)))
    levels = jnp.arange(LOOP_COUNT, dtype=jnp.int32)
    exit_own = own_slice(token_exit_loop)
    depth_own = jnp.sum((exit_own[:, None] == levels[None, :]).astype(f32), axis=0)

    normed_grad = scatter_mp(dot_cols(query_grad_b, q_full)) + dot_cols(pair_grad_b, kv_full)
    unused_first, attn_pull = jax.vjp(rms_norm, tokens_own, attention_norm_gain)
    inputs_norm_grad, attn_gain_part = attn_pull(normed_grad)
    tokens_grad = gather_mp(middle_grad + inputs_norm_grad).reshape(row_count, model_width)

    pair_grad_all = lax.all_gather(pair_grad_b, ("dp", "mp"), axis=0, tiled=True)
    small = sum_all(
        jnp.concatenate([attn_gain_part, mlp_gain_part, depth_own, confidence_own.reshape(1)])
    )
    kv_weight_grad = dot_rows(normed_cols, after(pair_grad_all, small))
    kv_weight_b = kv_weight_grad.astype(bf16)
    kv_lora_a = jnp.concatenate(
        [
            dot_cols(kv_weight_b[:, :HEAD_SIZE], kv_right[:, :HEAD_SIZE]),
            dot_cols(kv_weight_b[:, HEAD_SIZE:], kv_right[:, HEAD_SIZE:]),
        ],
        axis=1,
    )
    right_parts = jnp.concatenate(
        [
            qo_right,
            dot_rows(kv_left[:, :rank], kv_weight_b[:, :HEAD_SIZE]).astype(bf16),
            dot_rows(kv_left[:, rank:], kv_weight_b[:, HEAD_SIZE:]).astype(bf16),
        ],
        axis=1,
    )
    right_grads = jnp.sum(
        exchange(right_parts.reshape(dp_count, rank_own, -1)).astype(f32), axis=0
    )

    late_loop = after(current_loop, pair_grad_own)
    gate_weight_grad, gate_lora_a, gate_lora_b = receive_grad(
        late_loop, gate_up_sent, 0, block_all, gate_update_right, block_width
    )
    up_weight_grad, up_lora_a, up_lora_b = receive_grad(
        late_loop, gate_up_sent, 1, block_all, up_update_right, block_width
    )
    mlp_lora_a = sum_mp(jnp.concatenate([gate_lora_a, up_lora_a, down_lora_a], axis=1))

    gain_width = model_width // dp_count
    attn_gain_grad = lax.dynamic_slice_in_dim(small, dp_place * gain_width, gain_width, 0)
    mlp_gain_grad = lax.dynamic_slice_in_dim(
        small, model_width + dp_place * gain_width, gain_width, 0
    )
    counts = small[2 * model_width : 2 * model_width + LOOP_COUNT].astype(jnp.int32)
    confidence = small[2 * model_width + LOOP_COUNT :] / (row_count * dp_count)

    def place_loop(grad_item):
        chosen = jnp.arange(LOOP_COUNT)[:, None, None] == loop_selection
        return jnp.where(chosen, grad_item[None], 0.0)

    return (
        counts,
        confidence,
        mixed,
        tokens_grad,
        attn_gain_grad,
        mlp_gain_grad,
        q_weight_grad,
        kv_weight_grad,
        o_weight_grad,
        gate_weight_grad,
        up_weight_grad,
        down_weight_grad,
        place_loop(qo_lora_a[:, :rank]),
        place_loop(right_grads[:, :query_cols]),
        place_loop(kv_lora_a),
        place_loop(right_grads[:, 2 * query_cols :]),
        place_loop(qo_lora_a[:, rank:]),
        place_loop(right_grads[:, query_cols : 2 * query_cols]),
        place_loop(mlp_lora_a[:, :rank]),
        gate_lora_b,
        place_loop(mlp_lora_a[:, rank : 2 * rank]),
        up_lora_b,
        place_loop(mlp_lora_a[:, 2 * rank :]),
        down_lora_b,
    )


def solution(mesh):
    return jax.shard_map(
        body,
        mesh=mesh,
        in_specs=(
            P("dp", None),
            P("dp", None),
            P("dp"),
            P("dp"),
            P("dp"),
            P(),
            P(),
            P(),
            P(),
            P("dp", "mp"),
            P("dp", None),
            P("dp", "mp"),
            P("dp", "mp"),
            P("dp", "mp"),
            P("dp", "mp"),
            P(None, "dp", None),
            P(None, None, "mp"),
            P(None, "dp", None),
            P(),
            P(None, "dp", None),
            P(None, None, "mp"),
            P(None, "dp", None),
            P(None, None, "mp"),
            P(None, "dp", None),
            P(None, None, "mp"),
            P(None, "dp", None),
            P(None, None, "mp"),
        ),
        out_specs=(
            P(),
            P(),
            P("dp", None),
            P("dp", None),
            P("dp"),
            P("dp"),
            P("dp", "mp"),
            P("dp", None),
            P("dp", "mp"),
            P("dp", "mp"),
            P("dp", "mp"),
            P("dp", "mp"),
            P(None, "dp", None),
            P(None, "dp", "mp"),
            P(None, "dp", None),
            P(None, "dp", None),
            P(None, "dp", None),
            P(None, "dp", "mp"),
            P(None, "dp", None),
            P(None, "dp", "mp"),
            P(None, "dp", None),
            P(None, "dp", "mp"),
            P(None, "dp", None),
            P(None, "dp", "mp"),
        ),
        check_vma=False,
    )
```
